128 devices in a mesh: src: 2 (over z_lo), pen: 64 (over y, z_hi, x, core).
Axes of the slice: x: 4, y: 4, z: 4 (z_hi: 2, z_lo: 2; z = z_hi * 2 + z_lo), core: 2. Of those that a mesh axis runs over, the one named last changes fastest.
Arguments:
- permeability: float32 [128, 128, 128], P('pen'), may hold values from -6 to 6
- direction: float32 [128, 128, 128], P('pen'), may hold values from -6 to 6
- injection: float32 [2, 128, 128, 128], P('src', 'pen'), may hold values from -6 to 6
- lift_rock: float32 [32], replicated, may hold values from -6 to 6
- lift_well: float32 [32], replicated, may hold values from -6 to 6
- spectral: float32 [6912, 2, 32, 32], P('pen'), may hold values from -6 to 6
- pointwise: float32 [32, 32], replicated, may hold values from -1 to 1
- offsets: float32 [32], replicated, may hold values from -3 to 3
Outputs:
- gauss_newton: float32 [128, 128, 128], P('pen')
The draws below stay inside these ranges and needn't reach their ends.
All inputs are finite; a program needn't handle non-finite values.
Results may differ from the reference program's by a relative error of at most 0.0001.
Values sent between devices are 32-bit elements; how exact they have to be, the bound alone decides.
No kernel may reach another device: no remote copies, remote signals or barrier semaphores. Data moves between devices by JAX's collectives and lax.ppermute only.
A program may use at most 128 MiB of HBM per device.

```python
import math
import jax
import jax.numpy as jnp
from jax import lax

C = 32
MODES = 12
NX = 128
NY = 128
NZ = 128
SOURCES = 2
NMODES = 6912


def block_scale(own_key, shape, shards, least, top_value):
    def one(dim, blocks):
        heights = jax.random.uniform(jax.random.fold_in(jax.random.fold_in(own_key, 6), dim), (blocks,), jnp.float32, least / len(shards), top_value / len(shards))
        return jnp.repeat(jnp.exp(heights), shape[dim] // blocks).reshape((-1,) + (1,) * (len(shape) - dim - 1))

    factor_of = one(*shards[0])
    for cut in shards[1:]:
        factor_of = factor_of * one(*cut)
    return factor_of


def bell_draw(rng, shape, scale, reach, pieces=(), kind=jnp.bfloat16):
    gain = block_scale(rng, shape, pieces, -0.22, 0.18) if pieces else 1.0
    entries = jax.random.normal(rng, shape, jnp.float32) * scale * gain
    return jnp.minimum(jnp.maximum(entries, -reach), reach).astype(kind)


def setup_inputs(seed: int = 0) -> dict:
    key_of = jax.random.split(jax.random.key(seed), 9)
    return {
        "permeability": bell_draw(key_of[0], (NX, NY, NZ), 1.0, 6.0, ((0, 64),), jnp.float32),
        "direction": bell_draw(key_of[1], (NX, NY, NZ), 1.0, 6.0, ((0, 64),), jnp.float32),
        "injection": bell_draw(key_of[2], (SOURCES, NX, NY, NZ), 1.0, 6.0, ((0, 2), (1, 64)), jnp.float32),
        "lift_rock": bell_draw(key_of[3], (C,), 1 ** -0.5, 6.0, (), jnp.float32),
        "lift_well": bell_draw(key_of[4], (C,), 1 ** -0.5, 6.0, (), jnp.float32),
        "spectral": bell_draw(key_of[5], (NMODES, 2, C, C), ((NX * NY * NZ / (8 * MODES ** 3 * C)) ** 0.5), 6.0, ((0, 64),), jnp.float32),
        "pointwise": bell_draw(key_of[6], (C, C), C ** -0.5, 1.0, (), jnp.float32),
        "offsets": bell_draw(key_of[7], (C,), 0.5, 3.0, (), jnp.float32),
    }


highest = lax.Precision.HIGHEST

def contract(pattern, lefthand, righthand):
    return jnp.einsum(pattern, lefthand, righthand, precision=highest)

def phase_table(frequencies, length, offset, extent):
    positions = offset + jnp.arange(extent, dtype=jnp.int32)
    windings = jnp.mod(frequencies[:, None] * positions[None, :], length)
    angles = windings.astype(jnp.float32) * (2.0 * math.pi / length)
    return (jnp.cos(angles), jnp.sin(angles))

def make_tables(extent_x, extent_y, extent_z, kept_modes, offset, planes):
    ladder = jnp.arange(kept_modes, dtype=jnp.int32)
    signed = jnp.concatenate([ladder, ladder - 2 * kept_modes])
    cosine_outer, sine_outer = phase_table(signed, extent_x, offset, planes)
    cosine_middle, sine_middle = phase_table(signed, extent_y, 0, extent_y)
    cosine_inner, sine_inner = phase_table(ladder, extent_z, 0, extent_z)
    return (cosine_outer, sine_outer, cosine_middle, sine_middle, cosine_inner, sine_inner)

def depth_weights(kept_modes):
    ladder = jnp.arange(kept_modes, dtype=jnp.int32)
    return jnp.where(ladder == 0, 1.0, 2.0).astype(jnp.float32)

def forward(fields, tables, scaling):
    cosine_outer, sine_outer, cosine_middle, sine_middle, cosine_inner, sine_inner = tables
    members = fields.shape[0]
    inner_real = contract('bxyz,kz->bxyk', fields, cosine_inner)
    inner_imag = -contract('bxyz,kz->bxyk', fields, sine_inner)
    middle_real = contract('bxyk,jy->bxjk', inner_real, cosine_middle) + contract('bxyk,jy->bxjk', inner_imag, sine_middle)
    middle_imag = contract('bxyk,jy->bxjk', inner_imag, cosine_middle) - contract('bxyk,jy->bxjk', inner_real, sine_middle)
    outer_real = contract('bxjk,ix->ijkb', middle_real, cosine_outer) + contract('bxjk,ix->ijkb', middle_imag, sine_outer)
    outer_imag = contract('bxjk,ix->ijkb', middle_imag, cosine_outer) - contract('bxjk,ix->ijkb', middle_real, sine_outer)
    stacked = jnp.stack([outer_real, outer_imag], axis=3)
    return stacked.reshape(-1, 2, members) * scaling

def backward(spectra, tables, depth_scale, scaling):
    cosine_outer, sine_outer, cosine_middle, sine_middle, cosine_inner, sine_inner = tables
    members = spectra.shape[2]
    shaped = spectra.reshape(cosine_outer.shape[0], cosine_middle.shape[0], cosine_inner.shape[0], 2, members)
    shaped = shaped * depth_scale[None, None, :, None, None]
    real_part = shaped[:, :, :, 0]
    imag_part = shaped[:, :, :, 1]
    outer_real = contract('ijkb,ix->bxjk', real_part, cosine_outer) - contract('ijkb,ix->bxjk', imag_part, sine_outer)
    outer_imag = contract('ijkb,ix->bxjk', real_part, sine_outer) + contract('ijkb,ix->bxjk', imag_part, cosine_outer)
    middle_real = contract('bxjk,jy->bxyk', outer_real, cosine_middle) - contract('bxjk,jy->bxyk', outer_imag, sine_middle)
    middle_imag = contract('bxjk,jy->bxyk', outer_real, sine_middle) + contract('bxjk,jy->bxyk', outer_imag, cosine_middle)
    field = contract('bxyk,kz->bxyz', middle_real, cosine_inner) - contract('bxyk,kz->bxyz', middle_imag, sine_inner)
    return field * scaling

def mix(weights, spectra):
    weight_real = weights[:, 0]
    weight_imag = weights[:, 1]
    spec_real = spectra[:, 0]
    spec_imag = spectra[:, 1]
    out_real = contract('mio,msi->mso', weight_real, spec_real) - contract('mio,msi->mso', weight_imag, spec_imag)
    out_imag = contract('mio,msi->mso', weight_real, spec_imag) + contract('mio,msi->mso', weight_imag, spec_real)
    return jnp.stack([out_real, out_imag], axis=1)

def mix_adjoint(weights, spectra):
    weight_real = weights[:, 0]
    weight_imag = weights[:, 1]
    spec_real = spectra[:, 0]
    spec_imag = spectra[:, 1]
    in_real = contract('mio,mso->msi', weight_real, spec_real) + contract('mio,mso->msi', weight_imag, spec_imag)
    in_imag = contract('mio,mso->msi', weight_real, spec_imag) - contract('mio,mso->msi', weight_imag, spec_real)
    return jnp.stack([in_real, in_imag], axis=1)

def slope(values):
    return jax.grad(lambda inputs: jnp.sum(jax.nn.gelu(inputs)))(values)

def reference(permeability, direction, injection, lift_rock, lift_well, spectral, pointwise, offsets):
    tables = make_tables(NX, NY, NZ, MODES, 0, NX)
    scaling = 1.0 / math.sqrt(NX * NY * NZ)
    depth_scale = depth_weights(MODES)
    mode_scale = jnp.tile(depth_scale, 4 * MODES * MODES)
    inputs = jnp.concatenate([permeability[None], direction[None], injection], axis=0)
    spectra = forward(inputs, tables, scaling)
    lifted_spec = spectra[:, :, 0, None, None] * lift_rock + spectra[:, :, 2:, None] * lift_well
    coeffs = mix(spectral, lifted_spec)
    tangent_spec = mix(spectral, spectra[:, :, 1, None, None] * lift_rock)[:, :, 0]
    rock_weight = contract('io,i->o', pointwise, lift_rock)
    tangent = backward(tangent_spec, tables, depth_scale, scaling) + rock_weight[:, None, None, None] * direction[None]
    local_term = jnp.zeros_like(permeability)
    projected = jnp.zeros((spectra.shape[0], 2), jnp.float32)
    for source in range(SOURCES):
        lifted = lift_rock[:, None, None, None] * permeability[None] + lift_well[:, None, None, None] * injection[source][None]
        mixed_field = backward(coeffs[:, :, source], tables, depth_scale, scaling)
        mixed_field = mixed_field + contract('io,ixyz->oxyz', pointwise, lifted) + offsets[:, None, None, None]
        slopes = slope(mixed_field)
        adjoint = slopes * slopes * tangent
        local_term = local_term + contract('o,oxyz->xyz', rock_weight, adjoint)
        adjoint_spec = forward(adjoint, tables, scaling) * mode_scale[:, None, None]
        pulled = mix_adjoint(spectral, adjoint_spec[:, :, None, :])
        projected = projected + contract('mrsc,c->mr', pulled, lift_rock)
    through = backward(projected[:, :, None], tables, jnp.ones_like(depth_scale), scaling)[0]
    return through + local_term
```

```python
import math

import jax
import jax.numpy as jnp
import ml_dtypes
import numpy as np
from jax import lax
from jax.experimental import pallas as pl
from jax.experimental.pallas import tpu as pltpu
from jax.sharding import PartitionSpec as P

MODES = 12
GRID = 128
LANES = 128
BETAS = 8
KAPPAS = 8
OWNERS = BETAS * KAPPAS
CHANNELS = 32
CH = CHANNELS // KAPPAS
HALF = 24
F32 = jnp.float32
BF16 = jnp.bfloat16


def halves(table):
    top = np.asarray(table, np.float32).astype(ml_dtypes.bfloat16)
    rest = (np.asarray(table, np.float64) - top.astype(np.float64)).astype(np.float32)
    return top, rest.astype(ml_dtypes.bfloat16)


def signed(j):
    return np.where(j < MODES, j, j - 3 * MODES)


def build_tables():
    point = np.arange(GRID)
    angle = 2 * np.pi / GRID
    scale = 1.0 / math.sqrt(GRID**3)
    c = np.arange(MODES)
    weight = np.where(c == 0, 1.0, 2.0)
    cos_z = np.cos(angle * ((c[:, None] * point[None]) % GRID))
    sin_z = np.sin(angle * ((c[:, None] * point[None]) % GRID))
    b = np.arange(2 * MODES)
    turn = (signed(b)[:, None] * point[None]) % GRID
    cos_y, sin_y = np.cos(angle * turn), np.sin(angle * turn)
    re, im = slice(0, MODES), slice(MODES, HALF)

    za = np.zeros((GRID, 2 * LANES))
    za[:, 0:12], za[:, 12:24] = cos_z.T, -sin_z.T
    za[:, 128:140], za[:, 140:152] = -sin_z.T, -cos_z.T
    za *= scale

    order = (3 * np.arange(BETAS)[None, :] + np.arange(3)[:, None]).reshape(-1)
    ya = np.concatenate([cos_y[order], sin_y[order]], axis=1)

    x_of = (2 * np.arange(64)[None, :] + np.arange(2)[:, None]).reshape(-1)
    xb = np.zeros((BETAS, 2 * OWNERS, GRID))
    for beta in range(BETAS):
        for slot in range(64):
            j = (beta - 3 * slot) % 8
            if j < 3:
                a = (3 * slot + j) // 8
                ang = angle * ((signed(np.array(a)) * x_of) % GRID)
                xb[beta, slot], xb[beta, 64 + slot] = np.cos(ang), np.sin(ang)
    xi = xb.transpose(0, 2, 1).copy()

    eb = np.zeros((2 * LANES, 3, 2, LANES))
    for bi in range(3):
        for ch in range(CH):
            for k in range(MODES):
                lr, li = bi * HALF + k, bi * HALF + MODES + k
                hr, hi = ch * HALF + k, ch * HALF + MODES + k
                for lane in (hr, hi):
                    eb[lr, bi, 0, lane] = 1
                    eb[LANES + li, bi, 0, lane] = 1
                sign = {hr: -1, hi: 1}
                for lane in (hr, hi):
                    eb[li, bi, 1, lane] = sign[lane]
                    eb[LANES + lr, bi, 1, lane] = -sign[lane]
    eb = eb.reshape(2 * LANES, 6 * LANES)

    yc = np.zeros((2, 2, 2, GRID, BETAS, 2, 3, 2))
    for beta in range(BETAS):
        for bi in range(3):
            for plane in range(2):
                for field in range(2):
                    yc[plane, field, 0, :, beta, plane, bi, field] = cos_y[3 * beta + bi]
                    yc[plane, field, 1, :, beta, plane, bi, field] = sin_y[3 * beta + bi]
    yc = yc.reshape(8 * GRID, 12 * BETAS)

    zc = np.zeros((2, LANES, CH, GRID))
    zf = np.zeros((CH, GRID, 2, LANES))
    for ch in range(CH):
        at = ch * HALF
        r, i = slice(at, at + MODES), slice(at + MODES, at + HALF)
        zc[0, r, ch], zc[0, i, ch] = weight[:, None] * cos_z, -weight[:, None] * sin_z
        zc[1, r, ch], zc[1, i, ch] = -weight[:, None] * sin_z, -weight[:, None] * cos_z
        wc, ws = (weight[:, None] * cos_z).T, (weight[:, None] * sin_z).T
        zf[ch, :, 0, r], zf[ch, :, 0, i] = wc, -ws
        zf[ch, :, 1, r], zf[ch, :, 1, i] = -ws, -wc
    zc = zc.reshape(2 * LANES, CH * GRID) * scale
    zf = zf.reshape(CH * GRID, 2 * LANES) * scale

    ed = np.zeros((3, 2, LANES, 2, LANES))
    for bi in range(3):
        for ch in range(CH):
            for k in range(MODES):
                lr, li = bi * HALF + k, bi * HALF + MODES + k
                hr, hi = ch * HALF + k, ch * HALF + MODES + k
                ed[bi, 0, hr, 0, lr] = ed[bi, 0, hi, 0, lr] = 1
                ed[bi, 1, hr, 0, li], ed[bi, 1, hi, 0, li] = 1, -1
                ed[bi, 1, hr, 1, lr], ed[bi, 1, hi, 1, lr] = -1, 1
                ed[bi, 0, hr, 1, li] = ed[bi, 0, hi, 1, li] = 1
    ed = ed.reshape(6 * LANES, 2 * LANES)

    ye = np.zeros((3, 2, GRID, 2, BETAS, KAPPAS))
    ze = np.zeros((3, 2, LANES, GRID))
    for bi in range(3):
        for beta in range(BETAS):
            ye[bi, 0, :, :, beta, :] = cos_y[3 * beta + bi][:, None, None]
            ye[bi, 1, :, :, beta, :] = sin_y[3 * beta + bi][:, None, None]
        r, i = slice(bi * HALF, bi * HALF + MODES), slice(bi * HALF + MODES, (bi + 1) * HALF)
        ze[bi, 0, r], ze[bi, 0, i] = cos_z, -sin_z
        ze[bi, 1, r], ze[bi, 1, i] = -sin_z, -cos_z
    ye = ye.reshape(6 * GRID, 2 * OWNERS)
    ze = ze.reshape(6 * LANES, GRID) * scale

    return dict(
        za=halves(za), ya=halves(ya), xb=halves(xb), xi=halves(xi), yc=halves(yc),
        zc=halves(zc), zf=halves(zf), ye=halves(ye), ze=halves(ze),
        eb=eb.astype(ml_dtypes.bfloat16), ed=ed.astype(ml_dtypes.bfloat16),
    )


def split(x):
    top = x.astype(BF16)
    return top, (x - top.astype(F32)).astype(BF16)


def dot(a, b):
    return lax.dot_general(a, b, (((1,), (0,)), ((), ())), preferred_element_type=F32)


def left(table_hi, table_lo, x):
    hi, lo = split(x)
    return dot(table_hi, hi) + dot(table_hi, lo) + dot(table_lo, hi)


def right(x, table_hi, table_lo):
    hi, lo = split(x)
    return dot(hi, table_hi) + dot(lo, table_hi) + dot(hi, table_lo)


def right_exact(x, table):
    hi, lo = split(x)
    return dot(hi, table) + dot(lo, table)


def part_mask(shape):
    lane = lax.broadcasted_iota(jnp.int32, shape, 1)
    return lax.rem(lane, HALF) < MODES


def swap(x, real):
    return jnp.where(real, pltpu.roll(x, LANES - MODES, 1), pltpu.roll(x, MODES, 1))


def planes_kernel(p_ref, d_ref, i_ref, zh, zl, yh, yl, out_ref):
    x = jnp.concatenate([r[k] for r in (p_ref, d_ref, i_ref) for k in range(2)], axis=0)
    z = right(x, zh[...], zl[...])
    cols = [
        jnp.concatenate([z[k * GRID : (k + 1) * GRID, :LANES], z[k * GRID : (k + 1) * GRID, LANES:]], axis=0)
        for k in range(6)
    ]
    v = left(yh[...], yl[...], jnp.concatenate(cols, axis=1))
    for k in range(6):
        block = v[:, k * LANES : (k + 1) * LANES]
        total = block[0:8]
        for bi in (1, 2):
            total = total + pltpu.roll(block[8 * bi : 8 * bi + 8], HALF * bi, 1)
        out_ref[:, k, :] = total


def owners_kernel(beta_ref, r_ref, xbh, xbl, xih, xil, eb, out_ref):
    fields = [
        jnp.concatenate([r_ref[:, 2 * f, :], r_ref[:, 2 * f + 1, :]], axis=0) for f in range(3)
    ]
    g = left(xbh[0], xbl[0], jnp.concatenate(fields, axis=1))
    pre = [
        right_exact(
            jnp.concatenate(
                [g[:64, f * LANES : (f + 1) * LANES], g[64:, f * LANES : (f + 1) * LANES]], axis=1
            ),
            eb[...],
        )
        for f in range(3)
    ]
    real = part_mask((OWNERS, LANES))
    stack = []
    for bi in range(3):
        t, w = r_ref[:, 6 + bi, :], r_ref[:, 9 + bi, :]
        ts, ws = swap(t, real), swap(w, real)
        lo, mid, hi = 2 * bi * LANES, (2 * bi + 1) * LANES, (2 * bi + 2) * LANES
        coeff = (
            t * pre[0][:, lo:mid] + ts * pre[0][:, mid:hi]
            + w * pre[2][:, lo:mid] + ws * pre[2][:, mid:hi]
        )
        tangent = t * pre[1][:, lo:mid] + ts * pre[1][:, mid:hi]
        for q in (coeff, tangent):
            s = swap(q, real)
            stack.append(jnp.concatenate([q, jnp.where(real, -s, s)], axis=0))
    o = left(xih[0], xil[0], jnp.concatenate(stack, axis=1))
    for plane in range(2):
        for k in range(6):
            out_ref[:, plane * 6 + k, :] = o[plane * 64 : plane * 64 + 64, k * LANES : (k + 1) * LANES]


ROOT = math.sqrt(2.0 / math.pi)
CUBIC = 0.044715


def slope(x):
    square = x * x
    t = jnp.tanh(ROOT * x * (1.0 + CUBIC * square))
    return 0.5 * (1.0 + t) + 0.5 * ROOT * x * (1.0 - t * t) * (1.0 + 3.0 * CUBIC * square)


def field_kernel(
    scal, r_ref, p_ref, d_ref, i_ref, ych, ycl, zch, zcl, zfh, zfl, yfh, yfl,
    out_ref, local_ref, y_ref, z_ref,
):
    local_ref[...] = jnp.zeros_like(local_ref)

    def pair(kp, carry):
        rhs = jnp.concatenate(
            [
                jnp.concatenate([r_ref[beta * KAPPAS + 2 * kp + k] for beta in range(BETAS)], axis=0)
                for k in range(2)
            ],
            axis=1,
        )
        y_ref[...] = left(ych[...], ycl[...], rhs)
        for k in range(2):
            lanes = slice(k * LANES, (k + 1) * LANES)
            for plane in range(2):
                got = []
                for field in range(2):
                    base = (plane * 2 + field) * 2 * GRID
                    ab = jnp.concatenate(
                        [y_ref[base : base + GRID, lanes], y_ref[base + GRID : base + 2 * GRID, lanes]],
                        axis=1,
                    )
                    got.append(right(ab, zch[...], zcl[...]))
                perm, direc, inj = p_ref[plane], d_ref[plane], i_ref[plane]
                adj, local = [], local_ref[plane]
                for ch in range(CH):
                    o = (2 * kp + k) * CH + ch
                    rock = scal[0, o]
                    cells = slice(ch * GRID, (ch + 1) * GRID)
                    mixed = got[0][:, cells] + rock * perm + scal[1, o] * inj + scal[2, o]
                    s = slope(mixed)
                    a = s * s * (got[1][:, cells] + rock * direc)
                    local = local + rock * a
                    adj.append(a)
                local_ref[plane] = local
                z = right(jnp.concatenate(adj, axis=1), zfh[...], zfl[...])
                z_ref[2 * (2 * kp + k) + plane, :GRID] = z[:, :LANES]
                z_ref[2 * (2 * kp + k) + plane, GRID:] = z[:, LANES:]
        return carry

    lax.fori_loop(0, KAPPAS // 2, pair, 0)
    v = left(yfh[...], yfl[...], jnp.concatenate([z_ref[k] for k in range(2 * KAPPAS)], axis=1))
    for kappa in range(KAPPAS):
        for plane in range(2):
            at = (2 * kappa + plane) * LANES
            for bi in range(3):
                out_ref[:, kappa, plane * 3 + bi, :] = v[8 * bi : 8 * bi + 8, at : at + LANES]


def pull_kernel(beta_ref, r_ref, t_ref, xbh, xbl, xih, xil, ed, out_ref):
    fields = [
        jnp.concatenate([r_ref[:, bi, :], r_ref[:, 3 + bi, :]], axis=0) for bi in range(3)
    ]
    g = left(xbh[0], xbl[0], jnp.concatenate(fields, axis=1))
    real = part_mask((OWNERS, LANES))
    parts = []
    for bi in range(3):
        t = t_ref[:, 6 + bi, :]
        fr, fi = g[:64, bi * LANES : (bi + 1) * LANES], g[64:, bi * LANES : (bi + 1) * LANES]
        s = swap(fi, real)
        v = fr + jnp.where(real, s, -s)
        parts += [t * v, t * swap(v, real)]
    q = right_exact(jnp.concatenate(parts, axis=1), ed[...])
    h = left(xih[0], xil[0], jnp.concatenate([q[:, :LANES], q[:, LANES:]], axis=0))
    for plane in range(2):
        out_ref[:, plane, :] = h[plane * 64 : plane * 64 + 64]


def final_kernel(r_ref, mine_ref, theirs_ref, yh, yl, zh, zl, out_ref):
    g = left(yh[...], yl[...], jnp.concatenate([r_ref[:, 0, :], r_ref[:, 1, :]], axis=1))
    for plane in range(2):
        rows = jnp.concatenate(
            [g[k * GRID : (k + 1) * GRID, plane * LANES : (plane + 1) * LANES] for k in range(6)], axis=1
        )
        out_ref[plane] = right(rows, zh[...], zl[...]) + (mine_ref[plane] + theirs_ref[plane])


VMEM = pl.BlockSpec(memory_space=pltpu.VMEM)
SMEM = pl.BlockSpec(memory_space=pltpu.SMEM)
PARAMS = dict(compiler_params=pltpu.CompilerParams(vmem_limit_bytes=40 * 1024 * 1024))


def whole(shape):
    return pl.BlockSpec(shape, lambda i, beta: (0,) * len(shape))


def by_beta(shape):
    return pl.BlockSpec((1,) + shape, lambda i, beta: (beta[0], 0, 0))


def shards(permeability, direction, injection, lift_rock, lift_well, spectral, pointwise, offsets):
    tab = {
        k: tuple(jnp.asarray(x) for x in v) if isinstance(v, tuple) else jnp.asarray(v)
        for k, v in TABLES.items()
    }
    pen = lax.axis_index("pen")
    beta = (pen // KAPPAS).astype(jnp.int32).reshape(1)
    inj = injection[0]

    folded = jnp.stack(
        [
            jnp.sum(spectral * lift_rock[None, None, :, None], axis=2),
            jnp.sum(spectral * lift_well[None, None, :, None], axis=2),
        ]
    )
    folded = folded.reshape(2, 3, 3, MODES, 2, KAPPAS, CH).transpose(1, 5, 0, 2, 6, 4, 3)
    folded = folded.reshape(3, KAPPAS, 6, CH * HALF)
    folded = jnp.pad(folded, ((0, 5), (0, 0), (0, 0), (0, LANES - CH * HALF)))
    folded = jnp.roll(folded, lax.rem(3 * pen, BETAS), axis=0)

    spec_planes = pl.pallas_call(
        planes_kernel,
        out_shape=jax.ShapeDtypeStruct((BETAS, 6, LANES), F32),
        in_specs=[VMEM] * 7,
        out_specs=VMEM,
        name="planes",
        **PARAMS,
    )(permeability, direction, inj, *tab["za"], *tab["ya"])
    send = jnp.concatenate(
        [jnp.broadcast_to(spec_planes[:, None], (BETAS, KAPPAS, 6, LANES)), folded], axis=2
    ).reshape(OWNERS, 12, LANES)
    owned = lax.all_to_all(send, "pen", 0, 0, tiled=True)

    square = (2 * OWNERS, GRID)
    send = pl.pallas_call(
        owners_kernel,
        out_shape=jax.ShapeDtypeStruct((OWNERS, 12, LANES), F32),
        grid_spec=pltpu.PrefetchScalarGridSpec(
            num_scalar_prefetch=1,
            grid=(1,),
            in_specs=[whole((OWNERS, 12, LANES))] + [by_beta(square)] * 4 + [whole((2 * LANES, 6 * LANES))],
            out_specs=whole((OWNERS, 12, LANES)),
        ),
        name="owners",
        **PARAMS,
    )(beta, owned, *tab["xb"], *tab["xi"], tab["eb"])
    got = lax.all_to_all(send, "pen", 0, 0, tiled=True)

    rock = jnp.sum(pointwise * lift_rock[:, None], axis=0)
    well = jnp.sum(pointwise * lift_well[:, None], axis=0)
    scal = jnp.stack([rock, well, offsets])
    send, local = pl.pallas_call(
        field_kernel,
        out_shape=[
            jax.ShapeDtypeStruct((BETAS, KAPPAS, 6, LANES), F32),
            jax.ShapeDtypeStruct((2, GRID, GRID), F32),
        ],
        in_specs=[SMEM] + [VMEM] * 12,
        out_specs=[VMEM] * 2,
        scratch_shapes=[
            pltpu.VMEM((8 * GRID, 2 * LANES), F32),
            pltpu.VMEM((2 * KAPPAS, 2 * GRID, LANES), F32),
        ],
        name="field",
        **PARAMS,
    )(scal, got, permeability, direction, inj, *tab["yc"], *tab["zc"], *tab["zf"], *tab["ya"])
    theirs = lax.ppermute(local, "src", [(0, 1), (1, 0)])
    back = lax.all_to_all(send.reshape(OWNERS, 6, LANES), "pen", 0, 0, tiled=True)

    send = pl.pallas_call(
        pull_kernel,
        out_shape=jax.ShapeDtypeStruct((OWNERS, 2, LANES), F32),
        grid_spec=pltpu.PrefetchScalarGridSpec(
            num_scalar_prefetch=1,
            grid=(1,),
            in_specs=[whole((OWNERS, 6, LANES)), whole((OWNERS, 12, LANES))]
            + [by_beta(square)] * 4
            + [whole((6 * LANES, 2 * LANES))],
            out_specs=whole((OWNERS, 2, LANES)),
        ),
        name="pull",
        **PARAMS,
    )(beta, back, owned, *tab["xb"], *tab["xi"], tab["ed"])
    send = jnp.concatenate([send, send], axis=0)
    last = lax.all_to_all(send, ("src", "pen"), 0, 0, tiled=True)

    return pl.pallas_call(
        final_kernel,
        out_shape=jax.ShapeDtypeStruct((2, GRID, GRID), F32),
        in_specs=[VMEM] * 7,
        out_specs=VMEM,
        name="final",
        **PARAMS,
    )(last, local, theirs, *tab["ye"], *tab["ze"])


TABLES = build_tables()


def solution(mesh):
    placed = (
        P("pen", None, None),
        P("pen", None, None),
        P("src", "pen", None, None),
        P(),
        P(),
        P("pen", None, None, None),
        P(),
        P(),
    )
    return jax.shard_map(
        shards, mesh=mesh, in_specs=placed, out_specs=P("pen", None, None), check_vma=False
    )
```

```python
import math

import jax
import jax.numpy as jnp
import ml_dtypes
import numpy as np
from jax import lax
from jax.experimental import pallas as pl
from jax.experimental.pallas import tpu as pltpu
from jax.sharding import PartitionSpec as P

MODES = 12
GRID = 128
LANES = 128
BETAS = 8
KAPPAS = 8
OWNERS = BETAS * KAPPAS
CHANNELS = 32
CH = CHANNELS // KAPPAS
HALF = 24
PAIR = 48
FIELD_ROWS = 864
F32 = jnp.float32
BF16 = jnp.bfloat16


def halves(table):
    top = np.asarray(table, np.float32).astype(ml_dtypes.bfloat16)
    rest = (np.asarray(table, np.float64) - top.astype(np.float64)).astype(np.float32)
    return top, rest.astype(ml_dtypes.bfloat16)


def signed(j):
    return np.where(j < MODES, j, j - 3 * MODES)


def build_tables():
    point = np.arange(GRID)
    angle = 2 * np.pi / GRID
    scale = 1.0 / math.sqrt(GRID**3)
    c = np.arange(MODES)
    weight = np.where(c == 0, 1.0, 2.0)
    cos_z = np.cos(angle * ((c[:, None] * point[None]) % GRID))
    sin_z = np.sin(angle * ((c[:, None] * point[None]) % GRID))
    b = np.arange(2 * MODES)
    turn = (signed(b)[:, None] * point[None]) % GRID
    cos_y, sin_y = np.cos(angle * turn), np.sin(angle * turn)
    re, im = slice(0, MODES), slice(MODES, HALF)

    za = np.zeros((GRID, 2 * LANES))
    za[:, 0:12], za[:, 12:24] = cos_z.T, -sin_z.T
    za[:, 128:140], za[:, 140:152] = -sin_z.T, -cos_z.T
    za *= scale

    order = (3 * np.arange(BETAS)[None, :] + np.arange(3)[:, None]).reshape(-1)
    ya = np.concatenate([cos_y[order], sin_y[order]], axis=1)

    first = np.zeros((320, 2 * LANES), ml_dtypes.bfloat16)
    first[0:128], first[128:256] = halves(za)
    first[256:280], first[288:312] = halves(ya)

    x_of = (2 * np.arange(64)[None, :] + np.arange(2)[:, None]).reshape(-1)
    xb = np.zeros((BETAS, 2 * OWNERS, GRID))
    for beta in range(BETAS):
        for slot in range(64):
            j = (beta - 3 * slot) % 8
            if j < 3:
                a = (3 * slot + j) // 8
                ang = angle * ((signed(np.array(a)) * x_of) % GRID)
                xb[beta, slot], xb[beta, 64 + slot] = np.cos(ang), np.sin(ang)
    xi = xb.transpose(0, 2, 1).copy()

    eb = np.zeros((2 * LANES, 3, 2, LANES))
    for bi in range(3):
        for ch in range(CH):
            for k in range(MODES):
                lr, li = bi * HALF + k, bi * HALF + MODES + k
                hr, hi = ch * HALF + k, ch * HALF + MODES + k
                for lane in (hr, hi):
                    eb[lr, bi, 0, lane] = 1
                    eb[LANES + li, bi, 0, lane] = 1
                sign = {hr: -1, hi: 1}
                for lane in (hr, hi):
                    eb[li, bi, 1, lane] = sign[lane]
                    eb[LANES + lr, bi, 1, lane] = -sign[lane]
    eb = eb.reshape(2 * LANES, 6 * LANES)

    zc = np.zeros((LANES, 2, GRID))
    for q in range(2):
        r, i = slice(q * HALF, q * HALF + MODES), slice(q * HALF + MODES, (q + 1) * HALF)
        rs, js = slice(PAIR + r.start, PAIR + r.stop), slice(PAIR + i.start, PAIR + i.stop)
        zc[r, q], zc[i, q] = weight[:, None] * cos_z, -weight[:, None] * sin_z
        zc[rs, q], zc[js, q] = -weight[:, None] * sin_z, -weight[:, None] * cos_z
    zh, zl = halves(zc.reshape(LANES, 2 * GRID) * scale)
    yh, yl = halves(np.concatenate([cos_y[order], sin_y[order]], axis=0))
    field = np.zeros((FIELD_ROWS, 2 * GRID), ml_dtypes.bfloat16)
    field[0:128], field[128:256], field[256:384] = zh, zh, zl
    field[384:640, :LANES], field[384:640, LANES:] = zh.T, zl.T
    field[640:688, :GRID], field[640:688, GRID:] = yh, yh
    field[688:736, :GRID] = yl
    field[736:864, 0:48], field[736:864, 48:96], field[736:864, 96:144] = yh.T, yl.T, yh.T

    ed = np.zeros((3, 2, LANES, 2, LANES))
    for bi in range(3):
        for ch in range(CH):
            for k in range(MODES):
                lr, li = bi * HALF + k, bi * HALF + MODES + k
                hr, hi = ch * HALF + k, ch * HALF + MODES + k
                ed[bi, 0, hr, 0, lr] = ed[bi, 0, hi, 0, lr] = 1
                ed[bi, 1, hr, 0, li], ed[bi, 1, hi, 0, li] = 1, -1
                ed[bi, 1, hr, 1, lr], ed[bi, 1, hi, 1, lr] = -1, 1
                ed[bi, 0, hr, 1, li] = ed[bi, 0, hi, 1, li] = 1
    ed = ed.reshape(6 * LANES, 2 * LANES)

    ye = np.zeros((3, 2, GRID, 2, BETAS, KAPPAS))
    ze = np.zeros((3, 2, LANES, GRID))
    for bi in range(3):
        for beta in range(BETAS):
            ye[bi, 0, :, :, beta, :] = cos_y[3 * beta + bi][:, None, None]
            ye[bi, 1, :, :, beta, :] = sin_y[3 * beta + bi][:, None, None]
        r, i = slice(bi * HALF, bi * HALF + MODES), slice(bi * HALF + MODES, (bi + 1) * HALF)
        ze[bi, 0, r], ze[bi, 0, i] = cos_z, -sin_z
        ze[bi, 1, r], ze[bi, 1, i] = -sin_z, -cos_z
    ye = ye.reshape(6 * GRID, 2 * OWNERS)
    ze = ze.reshape(6 * LANES, GRID) * scale

    return dict(
        first=first, xb=halves(xb), xi=halves(xi), field=field, ye=halves(ye), ze=halves(ze),
        eb=eb.astype(ml_dtypes.bfloat16), ed=ed.astype(ml_dtypes.bfloat16),
    )


def split(x):
    top = x.astype(BF16)
    return top, (x - top.astype(F32)).astype(BF16)


def dot(a, b):
    return lax.dot_general(a, b, (((1,), (0,)), ((), ())), preferred_element_type=F32)


def left(table_hi, table_lo, x):
    hi, lo = split(x)
    return dot(table_hi, hi) + dot(table_hi, lo) + dot(table_lo, hi)


def right(x, table_hi, table_lo):
    hi, lo = split(x)
    return dot(hi, table_hi) + dot(lo, table_hi) + dot(hi, table_lo)


def right_exact(x, table):
    hi, lo = split(x)
    return dot(hi, table) + dot(lo, table)


def part_mask(shape):
    lane = lax.broadcasted_iota(jnp.int32, shape, 1)
    return lax.rem(lane, HALF) < MODES


def swap(x, real):
    return jnp.where(real, pltpu.roll(x, LANES - MODES, 1), pltpu.roll(x, MODES, 1))


def first_kernel(
    pen_ref, rock_ref, well_ref, s_hbm, p_hbm, d_hbm, i_hbm, tab_hbm, mix_hbm, off_hbm,
    out_ref, scal_ref, s_ref, p_ref, d_ref, i_ref, tab, mix_ref, off_ref, t_ref, sems,
):
    pairs = (
        (tab_hbm, tab), (p_hbm, p_ref), (d_hbm, d_ref), (i_hbm, i_ref),
        (mix_hbm, mix_ref), (off_hbm, off_ref), (s_hbm, s_ref),
    )
    copies = [pltpu.make_async_copy(src, dst, sems.at[k]) for k, (src, dst) in enumerate(pairs)]
    for copy in copies:
        copy.start()
    out_ref[:, :, 6:, :] = jnp.zeros((BETAS, KAPPAS, 6, LANES), F32)
    for copy in copies[:-1]:
        copy.wait()
    x = jnp.concatenate([r[k] for r in (p_ref, d_ref, i_ref) for k in range(2)], axis=0)
    z = right(x, tab[0:128], tab[128:256])
    cols = [
        jnp.concatenate([z[k * GRID : (k + 1) * GRID, :LANES], z[k * GRID : (k + 1) * GRID, LANES:]], axis=0)
        for k in range(6)
    ]
    v = left(tab[256:280], tab[288:312], jnp.concatenate(cols, axis=1))
    for k in range(6):
        col = v[:, k * LANES : (k + 1) * LANES]
        total = col[0:8]
        for bi in (1, 2):
            total = total + pltpu.roll(col[8 * bi : 8 * bi + 8], HALF * bi, 1)
        for kappa in range(KAPPAS):
            out_ref[:, kappa, k, :] = total

    rock = mix_ref[0:1] * rock_ref[0]
    well = mix_ref[0:1] * well_ref[0]
    for i in range(1, CHANNELS):
        rock = rock + mix_ref[i : i + 1] * rock_ref[i]
        well = well + mix_ref[i : i + 1] * well_ref[i]
    scal_ref[0:1], scal_ref[1:2], scal_ref[2:3] = rock, well, off_ref[...]

    copies[-1].wait()
    for part in range(2):
        rock = s_ref[part, 0] * rock_ref[0]
        well = s_ref[part, 0] * well_ref[0]
        for i in range(1, CHANNELS):
            x = s_ref[part, i]
            rock = rock + x * rock_ref[i]
            well = well + x * well_ref[i]
        t_ref[part, :, : rock.shape[1]] = rock
        t_ref[2 + part, :, : rock.shape[1]] = well
    lane = lax.broadcasted_iota(jnp.int32, (KAPPAS, LANES), 1)
    block = [[jnp.zeros((KAPPAS, LANES), F32) for _ in range(9)] for _ in range(2)]
    for ch in range(CH):
        for part in range(2):
            slot = 2 * ch + part
            inside = (lane >= slot * MODES) & (lane < (slot + 1) * MODES)
            for kind in range(2):
                x = t_ref[2 * kind + part, pl.ds(ch, KAPPAS, stride=CH), :]
                for row in range(9):
                    shift = ((slot - row) * MODES) % LANES
                    moved = pltpu.roll(x, shift, 1) if shift else x
                    block[kind][row] = jnp.where(inside, moved, block[kind][row])
    for j in range(3):
        beta = lax.rem(3 * pen_ref[0] + j, BETAS)
        for kind in range(2):
            for bi in range(3):
                out_ref[beta, :, 6 + 3 * kind + bi, :] = block[kind][3 * j + bi]


def owners_kernel(beta_ref, r_ref, xbh, xbl, xih, xil, eb, out_ref):
    fields = [
        jnp.concatenate([r_ref[:, 2 * f, :], r_ref[:, 2 * f + 1, :]], axis=0) for f in range(3)
    ]
    g = left(xbh[0], xbl[0], jnp.concatenate(fields, axis=1))
    pre = [
        right_exact(
            jnp.concatenate(
                [g[:64, f * LANES : (f + 1) * LANES], g[64:, f * LANES : (f + 1) * LANES]], axis=1
            ),
            eb[...],
        )
        for f in range(3)
    ]
    real = part_mask((OWNERS, LANES))
    stack = []
    for bi in range(3):
        t, w = r_ref[:, 6 + bi, :], r_ref[:, 9 + bi, :]
        ts, ws = swap(t, real), swap(w, real)
        lo, mid, hi = 2 * bi * LANES, (2 * bi + 1) * LANES, (2 * bi + 2) * LANES
        coeff = (
            t * pre[0][:, lo:mid] + ts * pre[0][:, mid:hi]
            + w * pre[2][:, lo:mid] + ws * pre[2][:, mid:hi]
        )
        tangent = t * pre[1][:, lo:mid] + ts * pre[1][:, mid:hi]
        for q in (coeff, 0.25 * tangent):
            s = swap(q, real)
            stack.append(jnp.concatenate([q, jnp.where(real, -s, s)], axis=0))
    o = left(xih[0], xil[0], jnp.concatenate(stack, axis=1))
    for plane in range(2):
        for k in range(6):
            out_ref[:, plane * 6 + k, :] = o[plane * 64 : plane * 64 + 64, k * LANES : (k + 1) * LANES]


ROOT = math.sqrt(2.0 / math.pi)
CUBIC = 0.044715


def twice_slope(x):
    square = x * x
    t = jnp.tanh(x * (ROOT + (ROOT * CUBIC) * square))
    return (1.0 + t) * (1.0 + (x * (ROOT + (3.0 * ROOT * CUBIC) * square)) * (1.0 - t))


def field_kernel(
    scal_hbm, r_ref, tab, p_hbm, d_hbm, i_hbm, out_ref, local_ref, scal, p_ref, d_ref, i_ref, z_ref, w0, w1, t0, t1, u0, u1, sems
):
    copies = [
        pltpu.make_async_copy(src, dst, sems.at[k])
        for k, (src, dst) in enumerate(((scal_hbm, scal), (p_hbm, p_ref), (d_hbm, d_ref), (i_hbm, i_ref)))
    ]
    for copy in copies:
        copy.start()
    w_refs, t_refs, u_refs = (w0, w1), (t0, t1), (u0, u1)
    lane = lax.broadcasted_iota(jnp.int32, (HALF, LANES), 1)
    low, high = lane < PAIR, (lane >= PAIR) & (lane < 2 * PAIR)
    zero = jnp.zeros((HALF, LANES), F32)
    local_ref[...] = jnp.zeros_like(local_ref)
    for copy in copies:
        copy.wait()

    def front(k):
        kappas = [GROUP * k + m for m in range(GROUP)]
        w_ref = w_refs[k % 2]
        rhs = []
        for field in range(2):
            for plane in range(2):
                for kappa in kappas:
                    s = jnp.concatenate(
                        [r_ref[:, kappa, plane * 6 + bi * 2 + field, :] for bi in range(3)], axis=0
                    )
                    right_pair = pltpu.roll(s, PAIR, 1)
                    left_pair = pltpu.roll(s, LANES - PAIR, 1)
                    rhs.append(
                        jnp.concatenate([jnp.where(low, s, zero), jnp.where(high, right_pair, zero)], axis=0)
                    )
                    rhs.append(
                        jnp.concatenate([jnp.where(low, left_pair, zero), jnp.where(high, s, zero)], axis=0)
                    )
        count = len(rhs)
        top, rest = split(jnp.concatenate(rhs, axis=1))
        y = dot(tab[736:864, :144], jnp.concatenate([top, top, rest], axis=0))
        top, rest = split(y)
        both = jnp.concatenate(
            [
                jnp.concatenate([h[:, c * LANES : (c + 1) * LANES] for h in (top, rest)], axis=1)
                for c in range(count)
            ],
            axis=0,
        )
        w_ref[...] = dot(both, tab[0:256]) + dot(both[:, :LANES], tab[256:384])

    def back(k):
        kappas = [GROUP * k + m for m in range(GROUP)]
        w_ref, t_ref, u_ref = w_refs[k % 2], t_refs[k % 2], u_refs[k % 2]
        half = 4 * GROUP * GRID
        at = 0
        for plane in range(2):
            perm, direc, inj = p_ref[plane], d_ref[plane], i_ref[plane]
            local = local_ref[plane]
            for kappa in kappas:
                for pair in range(2):
                    adj = []
                    for q in range(2):
                        o = kappa * CH + 2 * pair + q
                        rock = scal[0, o]
                        cells = slice(q * GRID, (q + 1) * GRID)
                        mixed = w_ref[at : at + GRID, cells] + rock * perm + scal[1, o] * inj + scal[2, o]
                        g = twice_slope(mixed)
                        a = g * g * (w_ref[half + at : half + at + GRID, cells] + (0.25 * rock) * direc)
                        local = local + rock * a
                        adj.append(a)
                    top, rest = split(jnp.concatenate(adj, axis=1))
                    t_ref[at : at + GRID], u_ref[at : at + GRID] = top, rest
                    at += GRID
            local_ref[plane] = local
        both = dot(t_ref[...], tab[384:640])
        z = both[:, :LANES] + both[:, LANES:] + dot(u_ref[...], tab[384:640, :LANES])
        top, rest = split(z)
        at = 0
        for plane in range(2):
            for kappa in kappas:
                for pair in range(2):
                    z_ref[4 * kappa + 2 * plane + pair, :GRID] = top[at : at + GRID]
                    z_ref[4 * kappa + 2 * plane + pair, GRID:] = rest[at : at + GRID]
                    at += GRID

    steps = KAPPAS // GROUP
    front(0)
    for k in range(steps):
        if k + 1 < steps:
            front(k + 1)
        back(k)

    for kappa in range(KAPPAS):
        v = dot(tab[640:736], jnp.concatenate([z_ref[4 * kappa + k] for k in range(4)], axis=1))
        v = v[:48] + v[48:]
        for plane in range(2):
            first, second = (v[:, k * LANES : (k + 1) * LANES] for k in (2 * plane, 2 * plane + 1))
            w = jnp.where(
                low,
                first[:HALF] + pltpu.roll(first[HALF:], LANES - PAIR, 1),
                jnp.where(high, pltpu.roll(second[:HALF], PAIR, 1) + second[HALF:], zero),
            )
            for bi in range(3):
                out_ref[:, kappa, plane * 3 + bi, :] = w[8 * bi : 8 * bi + 8]


GROUP = 1


def pull_kernel(beta_ref, r_ref, t_ref, xbh, xbl, xih, xil, ed, out_ref):
    fields = [
        jnp.concatenate([r_ref[:, bi, :], r_ref[:, 3 + bi, :]], axis=0) for bi in range(3)
    ]
    g = left(xbh[0], xbl[0], jnp.concatenate(fields, axis=1))
    real = part_mask((OWNERS, LANES))
    parts = []
    for bi in range(3):
        t = t_ref[:, 6 + bi, :]
        fr, fi = g[:64, bi * LANES : (bi + 1) * LANES], g[64:, bi * LANES : (bi + 1) * LANES]
        s = swap(fi, real)
        v = fr + jnp.where(real, s, -s)
        parts += [t * v, t * swap(v, real)]
    q = right_exact(jnp.concatenate(parts, axis=1), ed[...])
    h = left(xih[0], xil[0], jnp.concatenate([q[:, :LANES], q[:, LANES:]], axis=0))
    for plane in range(2):
        for source in range(2):
            out_ref[64 * source : 64 * source + 64, plane, :] = h[plane * 64 : plane * 64 + 64]


def final_kernel(
    r_ref, yh, yl, zh, zl, mine_hbm, theirs_hbm, out_ref, mine_ref, theirs_ref, sems
):
    copies = [
        pltpu.make_async_copy(src, dst, sems.at[k])
        for k, (src, dst) in enumerate(((mine_hbm, mine_ref), (theirs_hbm, theirs_ref)))
    ]
    for copy in copies:
        copy.start()
    g = left(yh[...], yl[...], jnp.concatenate([r_ref[:, 0, :], r_ref[:, 1, :]], axis=1))
    for copy in copies:
        copy.wait()
    for plane in range(2):
        rows = jnp.concatenate(
            [g[k * GRID : (k + 1) * GRID, plane * LANES : (plane + 1) * LANES] for k in range(6)], axis=1
        )
        out_ref[plane] = right(rows, zh[...], zl[...]) + (mine_ref[plane] + theirs_ref[plane])


VMEM = pl.BlockSpec(memory_space=pltpu.VMEM)
SMEM = pl.BlockSpec(memory_space=pltpu.SMEM)
HBM = pl.BlockSpec(memory_space=pltpu.HBM)
PARAMS = dict(compiler_params=pltpu.CompilerParams(vmem_limit_bytes=40 * 1024 * 1024))


def whole(shape):
    return pl.BlockSpec(shape, lambda i, beta: (0,) * len(shape))


def by_beta(shape):
    return pl.BlockSpec((1,) + shape, lambda i, beta: (beta[0], 0, 0))


def field_call(*operands):
    return pl.pallas_call(
        field_kernel,
        out_shape=[
            jax.ShapeDtypeStruct((BETAS, KAPPAS, 6, LANES), F32),
            jax.ShapeDtypeStruct((2, GRID, GRID), F32),
        ],
        in_specs=[HBM, VMEM, VMEM, HBM, HBM, HBM],
        out_specs=[VMEM] * 2,
        scratch_shapes=[pltpu.SMEM((3, CHANNELS), F32)]
        + [pltpu.VMEM((2, GRID, GRID), F32)] * 3
        + [
            pltpu.VMEM((4 * KAPPAS, 2 * GRID, LANES), BF16),
            *[pltpu.VMEM((8 * GROUP * GRID, 2 * GRID), F32)] * 2,
            *[pltpu.VMEM((4 * GROUP * GRID, 2 * GRID), BF16)] * 4,
            pltpu.SemaphoreType.DMA((4,)),
        ],
        name="field",
        **PARAMS,
    )(*operands)


def shards(permeability, direction, injection, lift_rock, lift_well, spectral, pointwise, offsets):
    tab = {
        k: tuple(jnp.asarray(x) for x in v) if isinstance(v, tuple) else jnp.asarray(v)
        for k, v in TABLES.items()
    }
    pen = lax.axis_index("pen")
    beta = (pen // KAPPAS).astype(jnp.int32).reshape(1)
    inj = injection[0]

    send, scal = pl.pallas_call(
        first_kernel,
        out_shape=[
            jax.ShapeDtypeStruct((BETAS, KAPPAS, 12, LANES), F32),
            jax.ShapeDtypeStruct((3, CHANNELS), F32),
        ],
        in_specs=[SMEM] * 3 + [HBM] * 7,
        out_specs=[VMEM] * 2,
        scratch_shapes=[
            pltpu.VMEM((2, CHANNELS, CHANNELS, spectral.shape[0]), F32),
            *[pltpu.VMEM((2, GRID, GRID), F32)] * 3,
            pltpu.VMEM((320, 2 * LANES), BF16),
            pltpu.VMEM((CHANNELS, CHANNELS), F32),
            pltpu.VMEM((1, CHANNELS), F32),
            pltpu.VMEM((4, CHANNELS, LANES), F32),
            pltpu.SemaphoreType.DMA((7,)),
        ],
        name="first",
        compiler_params=pltpu.CompilerParams(vmem_limit_bytes=60 * 1024 * 1024),
    )(
        pen.astype(jnp.int32).reshape(1), lift_rock, lift_well, spectral.transpose(1, 2, 3, 0),
        permeability, direction, inj, tab["first"], pointwise, offsets.reshape(1, CHANNELS),
    )
    send = send.reshape(OWNERS, 12, LANES)
    owned = lax.all_to_all(send, "pen", 0, 0, tiled=True)

    square = (2 * OWNERS, GRID)
    send = pl.pallas_call(
        owners_kernel,
        out_shape=jax.ShapeDtypeStruct((OWNERS, 12, LANES), F32),
        grid_spec=pltpu.PrefetchScalarGridSpec(
            num_scalar_prefetch=1,
            grid=(1,),
            in_specs=[whole((OWNERS, 12, LANES))] + [by_beta(square)] * 4 + [whole((2 * LANES, 6 * LANES))],
            out_specs=whole((OWNERS, 12, LANES)),
        ),
        name="owners",
        **PARAMS,
    )(beta, owned, *tab["xb"], *tab["xi"], tab["eb"])
    got = lax.all_to_all(send, "pen", 0, 0, tiled=True)

    send, local = field_call(scal, got.reshape(BETAS, KAPPAS, 12, LANES), tab["field"], permeability, direction, inj)
    theirs = lax.ppermute(local, "src", [(0, 1), (1, 0)])
    back = lax.all_to_all(send.reshape(OWNERS, 6, LANES), "pen", 0, 0, tiled=True)

    send = pl.pallas_call(
        pull_kernel,
        out_shape=jax.ShapeDtypeStruct((2 * OWNERS, 2, LANES), F32),
        grid_spec=pltpu.PrefetchScalarGridSpec(
            num_scalar_prefetch=1,
            grid=(1,),
            in_specs=[whole((OWNERS, 6, LANES)), whole((OWNERS, 12, LANES))]
            + [by_beta(square)] * 4
            + [whole((6 * LANES, 2 * LANES))],
            out_specs=whole((2 * OWNERS, 2, LANES)),
        ),
        name="pull",
        **PARAMS,
    )(beta, back, owned, *tab["xb"], *tab["xi"], tab["ed"])
    last = lax.all_to_all(send, ("src", "pen"), 0, 0, tiled=True)

    return pl.pallas_call(
        final_kernel,
        out_shape=jax.ShapeDtypeStruct((2, GRID, GRID), F32),
        in_specs=[VMEM] * 5 + [HBM] * 2,
        out_specs=VMEM,
        scratch_shapes=[pltpu.VMEM((2, GRID, GRID), F32)] * 2 + [pltpu.SemaphoreType.DMA((2,))],
        name="final",
        **PARAMS,
    )(last, *tab["ye"], *tab["ze"], local, theirs)


TABLES = build_tables()


def solution(mesh):
    placed = (
        P("pen", None, None),
        P("pen", None, None),
        P("src", "pen", None, None),
        P(),
        P(),
        P("pen", None, None, None),
        P(),
        P(),
    )
    return jax.shard_map(
        shards, mesh=mesh, in_specs=placed, out_specs=P("pen", None, None), check_vma=False
    )
```

```python
import math

import jax
import jax.numpy as jnp
import ml_dtypes
import numpy as np
from jax import lax
from jax.experimental import pallas as pl
from jax.experimental.pallas import tpu as pltpu
from jax.sharding import PartitionSpec as P

MODES = 12
GRID = 128
LANES = 128
BETAS = 8
KAPPAS = 8
OWNERS = BETAS * KAPPAS
CHANNELS = 32
CH = CHANNELS // KAPPAS
HALF = 24
PAIR = 48
FIELD_ROWS = 864
F32 = jnp.float32
BF16 = jnp.bfloat16


def halves(table):
    top = np.asarray(table, np.float32).astype(ml_dtypes.bfloat16)
    rest = (np.asarray(table, np.float64) - top.astype(np.float64)).astype(np.float32)
    return top, rest.astype(ml_dtypes.bfloat16)


def signed(j):
    return np.where(j < MODES, j, j - 3 * MODES)


def build_tables():
    point = np.arange(GRID)
    angle = 2 * np.pi / GRID
    scale = 1.0 / math.sqrt(GRID**3)
    c = np.arange(MODES)
    weight = np.where(c == 0, 1.0, 2.0)
    cos_z = np.cos(angle * ((c[:, None] * point[None]) % GRID))
    sin_z = np.sin(angle * ((c[:, None] * point[None]) % GRID))
    b = np.arange(2 * MODES)
    turn = (signed(b)[:, None] * point[None]) % GRID
    cos_y, sin_y = np.cos(angle * turn), np.sin(angle * turn)
    re, im = slice(0, MODES), slice(MODES, HALF)

    za = np.zeros((GRID, 2 * LANES))
    za[:, 0:12], za[:, 12:24] = cos_z.T, -sin_z.T
    za[:, 128:140], za[:, 140:152] = -sin_z.T, -cos_z.T
    za *= scale

    order = (3 * np.arange(BETAS)[None, :] + np.arange(3)[:, None]).reshape(-1)
    ya = np.concatenate([cos_y[order], sin_y[order]], axis=1)

    first = np.zeros((320, 2 * LANES), ml_dtypes.bfloat16)
    first[0:128], first[128:256] = halves(za)
    first[256:280], first[288:312] = halves(ya)

    x_of = (2 * np.arange(64)[None, :] + np.arange(2)[:, None]).reshape(-1)
    xb = np.zeros((BETAS, 2 * OWNERS, GRID))
    for beta in range(BETAS):
        for slot in range(64):
            j = (beta - 3 * slot) % 8
            if j < 3:
                a = (3 * slot + j) // 8
                ang = angle * ((signed(np.array(a)) * x_of) % GRID)
                xb[beta, slot], xb[beta, 64 + slot] = np.cos(ang), np.sin(ang)
    xi = xb.transpose(0, 2, 1).copy()
    xp = xi.reshape(BETAS, 2, 64, 2 * OWNERS).transpose(0, 2, 1, 3).reshape(BETAS, GRID, 2 * OWNERS).copy()

    eb = np.zeros((2 * LANES, 3, 2, LANES))
    for bi in range(3):
        for ch in range(CH):
            for k in range(MODES):
                lr, li = bi * HALF + k, bi * HALF + MODES + k
                hr, hi = ch * HALF + k, ch * HALF + MODES + k
                for lane in (hr, hi):
                    eb[lr, bi, 0, lane] = 1
                    eb[LANES + li, bi, 0, lane] = 1
                sign = {hr: -1, hi: 1}
                for lane in (hr, hi):
                    eb[li, bi, 1, lane] = sign[lane]
                    eb[LANES + lr, bi, 1, lane] = -sign[lane]
    eb = eb.reshape(2 * LANES, 6 * LANES)

    zc = np.zeros((LANES, 2, GRID))
    for q in range(2):
        r, i = slice(q * HALF, q * HALF + MODES), slice(q * HALF + MODES, (q + 1) * HALF)
        rs, js = slice(PAIR + r.start, PAIR + r.stop), slice(PAIR + i.start, PAIR + i.stop)
        zc[r, q], zc[i, q] = weight[:, None] * cos_z, -weight[:, None] * sin_z
        zc[rs, q], zc[js, q] = -weight[:, None] * sin_z, -weight[:, None] * cos_z
    zh, zl = halves(zc.reshape(LANES, 2 * GRID) * scale)
    yh, yl = halves(np.concatenate([cos_y[order], sin_y[order]], axis=0))
    field = np.zeros((FIELD_ROWS, 2 * GRID), ml_dtypes.bfloat16)
    field[0:128], field[128:256], field[256:384] = zh, zh, zl
    field[384:640, :LANES], field[384:640, LANES:] = zh.T, zl.T
    field[640:688, :GRID], field[640:688, GRID:] = yh, yh
    field[688:736, :GRID] = yl
    field[736:864, 0:48], field[736:864, 48:96], field[736:864, 96:144] = yh.T, yl.T, yh.T

    ed = np.zeros((3, 2, LANES, 2, LANES))
    for bi in range(3):
        for ch in range(CH):
            for k in range(MODES):
                lr, li = bi * HALF + k, bi * HALF + MODES + k
                hr, hi = ch * HALF + k, ch * HALF + MODES + k
                ed[bi, 0, hr, 0, lr] = ed[bi, 0, hi, 0, lr] = 1
                ed[bi, 1, hr, 0, li], ed[bi, 1, hi, 0, li] = 1, -1
                ed[bi, 1, hr, 1, lr], ed[bi, 1, hi, 1, lr] = -1, 1
                ed[bi, 0, hr, 1, li] = ed[bi, 0, hi, 1, li] = 1
    ed = ed.reshape(6 * LANES, 2 * LANES)

    ze = np.zeros((LANES, 2, GRID))
    for q in range(2):
        at = q * PAIR
        ze[at : at + 12, q], ze[at + 12 : at + 24, q] = cos_z, -sin_z
        ze[at + 24 : at + 36, q], ze[at + 36 : at + 48, q] = -sin_z, -cos_z
    zh, zl = halves(ze.reshape(LANES, 2 * GRID) * scale)
    final = np.zeros((512, 2 * GRID), ml_dtypes.bfloat16)
    final[0:128], final[128:256], final[256:384] = zh, zh, zl
    final[384:512] = field[736:864]

    return dict(
        first=first, xb=halves(xb), xi=halves(xi), field=field, final=final, xp=halves(xp),
        eb=eb.astype(ml_dtypes.bfloat16), ed=ed.astype(ml_dtypes.bfloat16),
    )


def split(x):
    top = x.astype(BF16)
    return top, (x - top.astype(F32)).astype(BF16)


def dot(a, b):
    return lax.dot_general(a, b, (((1,), (0,)), ((), ())), preferred_element_type=F32)


def left(table_hi, table_lo, x):
    hi, lo = split(x)
    return dot(table_hi, hi) + dot(table_hi, lo) + dot(table_lo, hi)


def right(x, table_hi, table_lo):
    hi, lo = split(x)
    return dot(hi, table_hi) + dot(lo, table_hi) + dot(hi, table_lo)


def right_exact(x, table):
    hi, lo = split(x)
    return dot(hi, table) + dot(lo, table)


def part_mask(shape):
    lane = lax.broadcasted_iota(jnp.int32, shape, 1)
    return lax.rem(lane, HALF) < MODES


def swap(x, real):
    return jnp.where(real, pltpu.roll(x, LANES - MODES, 1), pltpu.roll(x, MODES, 1))


def first_kernel(
    pen_ref, rock_ref, well_ref, s_hbm, p_hbm, d_hbm, i_hbm, tab_hbm,
    out_ref, s_ref, p_ref, d_ref, i_ref, tab, t_ref, sems,
):
    pairs = (
        (tab_hbm, tab), (p_hbm, p_ref), (d_hbm, d_ref), (i_hbm, i_ref),
        (s_hbm, s_ref),
    )
    copies = [pltpu.make_async_copy(src, dst, sems.at[k]) for k, (src, dst) in enumerate(pairs)]
    for copy in copies:
        copy.start()
    for copy in copies[:-1]:
        copy.wait()
    x = jnp.concatenate([r[k] for r in (p_ref, d_ref, i_ref) for k in range(2)], axis=0)
    z = right(x, tab[0:128], tab[128:256])
    cols = [
        jnp.concatenate([z[k * GRID : (k + 1) * GRID, :LANES], z[k * GRID : (k + 1) * GRID, LANES:]], axis=0)
        for k in range(6)
    ]
    v = left(tab[256:280], tab[288:312], jnp.concatenate(cols, axis=1))
    lane = lax.broadcasted_iota(jnp.int32, (BETAS, LANES), 1)
    piece = [
        [v[8 * bi : 8 * bi + 8, k * LANES : (k + 1) * LANES] for bi in range(3)] for k in range(6)
    ]
    rows = [pltpu.roll(piece[k][2], 96, 1) for k in range(6)]
    for bi in range(2):
        for third in range(3):
            moved = pltpu.roll(piece[5][bi], 120 - 8 * third, 1)
            rows[3 * bi + third] = jnp.where(lane >= 120, moved, rows[3 * bi + third])
        total = piece[0][bi]
        for k in range(1, 5):
            total = total + pltpu.roll(piece[k][bi], HALF * k, 1)
        rows.append(total)
    for r in range(8):
        for kappa in range(KAPPAS):
            out_ref[kappa, :, r, :] = rows[r]

    copies[-1].wait()
    for part in range(2):
        rock = s_ref[part, 0] * rock_ref[0]
        well = s_ref[part, 0] * well_ref[0]
        for i in range(1, CHANNELS):
            x = s_ref[part, i]
            rock = rock + x * rock_ref[i]
            well = well + x * well_ref[i]
        t_ref[part, :, : rock.shape[1]] = rock
        t_ref[2 + part, :, : rock.shape[1]] = well
    lane = lax.broadcasted_iota(jnp.int32, (KAPPAS, LANES), 1)
    block = [[jnp.zeros((KAPPAS, LANES), F32) for _ in range(9)] for _ in range(2)]
    for ch in range(CH):
        for part in range(2):
            slot = 2 * ch + part
            inside = (lane >= slot * MODES) & (lane < (slot + 1) * MODES)
            for kind in range(2):
                x = t_ref[2 * kind + part, pl.ds(ch, KAPPAS, stride=CH), :]
                for row in range(9):
                    shift = ((slot - row) * MODES) % LANES
                    moved = pltpu.roll(x, shift, 1) if shift else x
                    block[kind][row] = jnp.where(inside, moved, block[kind][row])
    for j in range(3):
        beta = lax.rem(3 * pen_ref[0] + j, BETAS)
        for kind in range(2):
            for bi in range(3):
                r = 3 * kind + bi
                out_ref[:, beta, r, :] = out_ref[:, beta, r, :] + block[kind][3 * j + bi]


def owners_kernel(beta_ref, r_ref, xbh, xbl, xih, xil, eb, out_ref):
    raw = [r_ref[:, r, :] for r in range(8)]
    lane = lax.broadcasted_iota(jnp.int32, (OWNERS, LANES), 1)

    def take(x, source, target, width, base):
        shift = (target - source) % LANES
        moved = pltpu.roll(x, shift, 1) if shift else x
        return jnp.where((lane >= target) & (lane < target + width), moved, base)

    planes = []
    for k in range(6):
        x = take(raw[k], 96, 48, HALF, jnp.zeros((OWNERS, LANES), F32))
        for bi in range(2):
            if k < 5:
                x = take(raw[6 + bi], HALF * k, HALF * bi, HALF, x)
            else:
                for third in range(3):
                    x = take(raw[3 * bi + third], 120, HALF * bi + 8 * third, 8, x)
        planes.append(x)
    fields = [jnp.concatenate(planes[2 * f : 2 * f + 2], axis=0) for f in range(3)]
    g = left(xbh[0], xbl[0], jnp.concatenate(fields, axis=1))
    pre = [
        right_exact(
            jnp.concatenate(
                [g[:64, f * LANES : (f + 1) * LANES], g[64:, f * LANES : (f + 1) * LANES]], axis=1
            ),
            eb[...],
        )
        for f in range(3)
    ]
    real = part_mask((OWNERS, LANES))
    stack = []
    for bi in range(3):
        t, w = raw[bi], raw[3 + bi]
        ts, ws = swap(t, real), swap(w, real)
        lo, mid, hi = 2 * bi * LANES, (2 * bi + 1) * LANES, (2 * bi + 2) * LANES
        coeff = (
            t * pre[0][:, lo:mid] + ts * pre[0][:, mid:hi]
            + w * pre[2][:, lo:mid] + ws * pre[2][:, mid:hi]
        )
        tangent = t * pre[1][:, lo:mid] + ts * pre[1][:, mid:hi]
        for q in (coeff, 0.25 * tangent):
            s = swap(q, real)
            stack.append(jnp.concatenate([q, jnp.where(real, -s, s)], axis=0))
    o = left(xih[0], xil[0], jnp.concatenate(stack, axis=1))
    for plane in range(2):
        for k in range(6):
            out_ref[:, plane * 6 + k, :] = o[plane * 64 : plane * 64 + 64, k * LANES : (k + 1) * LANES]


ROOT = math.sqrt(2.0 / math.pi)
CUBIC = 0.044715


def twice_slope(x):
    square = x * x
    t = jnp.tanh(x * (ROOT + (ROOT * CUBIC) * square))
    return (1.0 + t) * (1.0 + (x * (ROOT + (3.0 * ROOT * CUBIC) * square)) * (1.0 - t))


def field_kernel(
    scal_hbm, r_ref, tab, p_hbm, d_hbm, i_hbm, out_ref, local_ref, scal, p_ref, d_ref, i_ref, z_ref, w0, w1, t0, t1, u0, u1, sems
):
    copies = [
        pltpu.make_async_copy(src, dst, sems.at[k])
        for k, (src, dst) in enumerate(((scal_hbm, scal), (p_hbm, p_ref), (d_hbm, d_ref), (i_hbm, i_ref)))
    ]
    for copy in copies:
        copy.start()
    w_refs, t_refs, u_refs = (w0, w1), (t0, t1), (u0, u1)
    lane = lax.broadcasted_iota(jnp.int32, (HALF, LANES), 1)
    low, high = lane < PAIR, (lane >= PAIR) & (lane < 2 * PAIR)
    zero = jnp.zeros((HALF, LANES), F32)
    local_ref[...] = jnp.zeros_like(local_ref)
    for copy in copies:
        copy.wait()

    def front(k):
        kappas = [GROUP * k + m for m in range(GROUP)]
        w_ref = w_refs[k % 2]
        rhs = []
        for field in range(2):
            for plane in range(2):
                for kappa in kappas:
                    s = jnp.concatenate(
                        [r_ref[kappa, :, plane * 6 + bi * 2 + field, :] for bi in range(3)], axis=0
                    )
                    right_pair = pltpu.roll(s, PAIR, 1)
                    left_pair = pltpu.roll(s, LANES - PAIR, 1)
                    rhs.append(
                        jnp.concatenate([jnp.where(low, s, zero), jnp.where(high, right_pair, zero)], axis=0)
                    )
                    rhs.append(
                        jnp.concatenate([jnp.where(low, left_pair, zero), jnp.where(high, s, zero)], axis=0)
                    )
        count = len(rhs)
        top, rest = split(jnp.concatenate(rhs, axis=1))
        y = dot(tab[736:864, :144], jnp.concatenate([top, top, rest], axis=0))
        top, rest = split(y)
        both = jnp.concatenate(
            [
                jnp.concatenate([h[:, c * LANES : (c + 1) * LANES] for h in (top, rest)], axis=1)
                for c in range(count)
            ],
            axis=0,
        )
        w_ref[...] = dot(both, tab[0:256]) + dot(both[:, :LANES], tab[256:384])

    def back(k):
        kappas = [GROUP * k + m for m in range(GROUP)]
        w_ref, t_ref, u_ref = w_refs[k % 2], t_refs[k % 2], u_refs[k % 2]
        half = 4 * GROUP * GRID
        at = 0
        for plane in range(2):
            perm, direc, inj = p_ref[plane], d_ref[plane], i_ref[plane]
            local = local_ref[plane]
            for kappa in kappas:
                for pair in range(2):
                    adj = []
                    for q in range(2):
                        o = kappa * CH + 2 * pair + q
                        rock = scal[0, o]
                        cells = slice(q * GRID, (q + 1) * GRID)
                        mixed = w_ref[at : at + GRID, cells] + rock * perm + scal[1, o] * inj + scal[2, o]
                        g = twice_slope(mixed)
                        a = g * g * (w_ref[half + at : half + at + GRID, cells] + (0.25 * rock) * direc)
                        local = local + rock * a
                        adj.append(a)
                    top, rest = split(jnp.concatenate(adj, axis=1))
                    t_ref[at : at + GRID], u_ref[at : at + GRID] = top, rest
                    at += GRID
            local_ref[plane] = local
        both = dot(t_ref[...], tab[384:640])
        z = both[:, :LANES] + both[:, LANES:] + dot(u_ref[...], tab[384:640, :LANES])
        top, rest = split(z)
        at = 0
        for plane in range(2):
            for kappa in kappas:
                for pair in range(2):
                    z_ref[4 * kappa + 2 * plane + pair, :GRID] = top[at : at + GRID]
                    z_ref[4 * kappa + 2 * plane + pair, GRID:] = rest[at : at + GRID]
                    at += GRID

    steps = KAPPAS // GROUP
    front(0)
    for k in range(steps):
        if k + 1 < steps:
            front(k + 1)
        back(k)

    for kappa in range(KAPPAS):
        v = dot(tab[640:736], jnp.concatenate([z_ref[4 * kappa + k] for k in range(4)], axis=1))
        v = v[:48] + v[48:]
        for plane in range(2):
            first, second = (v[:, k * LANES : (k + 1) * LANES] for k in (2 * plane, 2 * plane + 1))
            w = jnp.where(
                low,
                first[:HALF] + pltpu.roll(first[HALF:], LANES - PAIR, 1),
                jnp.where(high, pltpu.roll(second[:HALF], PAIR, 1) + second[HALF:], zero),
            )
            for bi in range(3):
                out_ref[kappa, :, plane * 3 + bi, :] = w[8 * bi : 8 * bi + 8]


GROUP = 1


def pull_kernel(beta_ref, r_ref, t_ref, xbh, xbl, xih, xil, ed, out_ref):
    fields = [
        jnp.concatenate([r_ref[:, bi, :], r_ref[:, 3 + bi, :]], axis=0) for bi in range(3)
    ]
    g = left(xbh[0], xbl[0], jnp.concatenate(fields, axis=1))
    real = part_mask((OWNERS, LANES))
    parts = []
    for bi in range(3):
        t = t_ref[:, bi, :]
        fr, fi = g[:64, bi * LANES : (bi + 1) * LANES], g[64:, bi * LANES : (bi + 1) * LANES]
        s = swap(fi, real)
        v = fr + jnp.where(real, s, -s)
        parts += [t * v, t * swap(v, real)]
    q = right_exact(jnp.concatenate(parts, axis=1), ed[...])
    h = left(xih[0], xil[0], jnp.concatenate([q[:, :LANES], q[:, LANES:]], axis=0))
    for source in range(2):
        out_ref[GRID * source : GRID * source + GRID] = h


def final_kernel(r_ref, tab, mine_hbm, theirs_hbm, out_ref, mine_ref, theirs_ref, sems):
    copies = [
        pltpu.make_async_copy(src, dst, sems.at[k])
        for k, (src, dst) in enumerate(((mine_hbm, mine_ref), (theirs_hbm, theirs_ref)))
    ]
    for copy in copies:
        copy.start()
    lane = lax.broadcasted_iota(jnp.int32, (BETAS, LANES), 1)
    rows = [[], []]
    total = []
    for plane in range(2):
        x = r_ref[pl.ds(plane, BETAS, stride=2), :]
        for k in range(1, 2 * KAPPAS):
            x = x + r_ref[pl.ds(2 * BETAS * k + plane, BETAS, stride=2), :]
        total.append(x)
    for part in range(2):
        for bi in range(3):
            x = jnp.zeros((BETAS, LANES), F32)
            for plane in range(2):
                at = plane * PAIR + part * HALF
                shift = (at - HALF * bi) % LANES
                moved = pltpu.roll(total[plane], shift, 1) if shift else total[plane]
                x = jnp.where((lane >= at) & (lane < at + HALF), moved, x)
            rows[part].append(x)
    top, rest = split(jnp.concatenate(rows[0] + rows[1], axis=0))
    y = dot(tab[384:512, :144], jnp.concatenate([top, top, rest], axis=0))
    top, rest = split(y)
    z = dot(jnp.concatenate([top, rest], axis=1), tab[0:256]) + dot(top, tab[256:384])
    for copy in copies:
        copy.wait()
    for plane in range(2):
        out_ref[plane] = z[:, plane * GRID : (plane + 1) * GRID] + (mine_ref[plane] + theirs_ref[plane])


VMEM = pl.BlockSpec(memory_space=pltpu.VMEM)
SMEM = pl.BlockSpec(memory_space=pltpu.SMEM)
HBM = pl.BlockSpec(memory_space=pltpu.HBM)
PARAMS = dict(compiler_params=pltpu.CompilerParams(vmem_limit_bytes=40 * 1024 * 1024))


def whole(shape):
    return pl.BlockSpec(shape, lambda i, beta: (0,) * len(shape))


def by_beta(shape):
    return pl.BlockSpec((1,) + shape, lambda i, beta: (beta[0], 0, 0))


def field_call(*operands):
    return pl.pallas_call(
        field_kernel,
        out_shape=[
            jax.ShapeDtypeStruct((KAPPAS, BETAS, 6, LANES), F32),
            jax.ShapeDtypeStruct((2, GRID, GRID), F32),
        ],
        in_specs=[HBM, VMEM, VMEM, HBM, HBM, HBM],
        out_specs=[VMEM] * 2,
        scratch_shapes=[pltpu.SMEM((3, CHANNELS), F32)]
        + [pltpu.VMEM((2, GRID, GRID), F32)] * 3
        + [
            pltpu.VMEM((4 * KAPPAS, 2 * GRID, LANES), BF16),
            *[pltpu.VMEM((8 * GROUP * GRID, 2 * GRID), F32)] * 2,
            *[pltpu.VMEM((4 * GROUP * GRID, 2 * GRID), BF16)] * 4,
            pltpu.SemaphoreType.DMA((4,)),
        ],
        name="field",
        **PARAMS,
    )(*operands)


def shards(permeability, direction, injection, lift_rock, lift_well, spectral, pointwise, offsets):
    tab = {
        k: tuple(jnp.asarray(x) for x in v) if isinstance(v, tuple) else jnp.asarray(v)
        for k, v in TABLES.items()
    }
    pen = lax.axis_index("pen")
    beta = lax.rem(pen, BETAS).astype(jnp.int32).reshape(1)
    inj = injection[0]

    send = pl.pallas_call(
        first_kernel,
        out_shape=jax.ShapeDtypeStruct((KAPPAS, BETAS, 8, LANES), F32),
        in_specs=[SMEM] * 3 + [HBM] * 5,
        out_specs=VMEM,
        scratch_shapes=[
            pltpu.VMEM((2, CHANNELS, CHANNELS, spectral.shape[0]), F32),
            *[pltpu.VMEM((2, GRID, GRID), F32)] * 3,
            pltpu.VMEM((320, 2 * LANES), BF16),
            pltpu.VMEM((4, CHANNELS, LANES), F32),
            pltpu.SemaphoreType.DMA((5,)),
        ],
        name="first",
        compiler_params=pltpu.CompilerParams(vmem_limit_bytes=60 * 1024 * 1024),
    )(
        pen.astype(jnp.int32).reshape(1), lift_rock, lift_well, spectral.transpose(1, 2, 3, 0),
        permeability, direction, inj, tab["first"],
    )
    send = send.reshape(OWNERS, 8, LANES)
    owned = lax.all_to_all(send, "pen", 0, 0, tiled=True)

    square = (2 * OWNERS, GRID)
    send = pl.pallas_call(
        owners_kernel,
        out_shape=jax.ShapeDtypeStruct((OWNERS, 12, LANES), F32),
        grid_spec=pltpu.PrefetchScalarGridSpec(
            num_scalar_prefetch=1,
            grid=(1,),
            in_specs=[whole((OWNERS, 8, LANES))] + [by_beta(square)] * 4 + [whole((2 * LANES, 6 * LANES))],
            out_specs=whole((OWNERS, 12, LANES)),
        ),
        name="owners",
        **PARAMS,
    )(beta, owned, *tab["xb"], *tab["xi"], tab["eb"])
    got = lax.all_to_all(send, "pen", 0, 0, tiled=True)

    rock = jnp.sum(pointwise * lift_rock[:, None], axis=0)
    well = jnp.sum(pointwise * lift_well[:, None], axis=0)
    scal = jnp.stack([rock, well, offsets])
    send, local = field_call(scal, got.reshape(KAPPAS, BETAS, 12, LANES), tab["field"], permeability, direction, inj)
    theirs = lax.ppermute(local, "src", [(0, 1), (1, 0)])
    back = lax.all_to_all(send.reshape(OWNERS, 6, LANES), "pen", 0, 0, tiled=True)

    send = pl.pallas_call(
        pull_kernel,
        out_shape=jax.ShapeDtypeStruct((4 * OWNERS, LANES), F32),
        grid_spec=pltpu.PrefetchScalarGridSpec(
            num_scalar_prefetch=1,
            grid=(1,),
            in_specs=[whole((OWNERS, 6, LANES)), whole((OWNERS, 8, LANES))]
            + [by_beta(square)] * 4
            + [whole((6 * LANES, 2 * LANES))],
            out_specs=whole((4 * OWNERS, LANES)),
        ),
        name="pull",
        **PARAMS,
    )(beta, back, owned, *tab["xb"], *tab["xp"], tab["ed"])
    last = lax.all_to_all(send, ("src", "pen"), 0, 0, tiled=True)

    return pl.pallas_call(
        final_kernel,
        out_shape=jax.ShapeDtypeStruct((2, GRID, GRID), F32),
        in_specs=[VMEM] * 2 + [HBM] * 2,
        out_specs=VMEM,
        scratch_shapes=[pltpu.VMEM((2, GRID, GRID), F32)] * 2 + [pltpu.SemaphoreType.DMA((2,))],
        name="final",
        **PARAMS,
    )(last, tab["final"], local, theirs)


TABLES = build_tables()


def solution(mesh):
    placed = (
        P("pen", None, None),
        P("pen", None, None),
        P("src", "pen", None, None),
        P(),
        P(),
        P("pen", None, None, None),
        P(),
        P(),
    )
    return jax.shard_map(
        shards, mesh=mesh, in_specs=placed, out_specs=P("pen", None, None), check_vma=False
    )
```

```python
import math

import jax
import jax.numpy as jnp
import ml_dtypes
import numpy as np
from jax import lax
from jax.experimental import pallas as pl
from jax.experimental.pallas import tpu as pltpu
from jax.sharding import PartitionSpec as P

MODES = 12
GRID = 128
LANES = 128
BETAS = 8
KAPPAS = 8
OWNERS = BETAS * KAPPAS
CHANNELS = 32
CH = CHANNELS // KAPPAS
HALF = 24
PAIR = 48
FIELD_ROWS = 864
F32 = jnp.float32
BF16 = jnp.bfloat16


def halves(table):
    top = np.asarray(table, np.float32).astype(ml_dtypes.bfloat16)
    rest = (np.asarray(table, np.float64) - top.astype(np.float64)).astype(np.float32)
    return top, rest.astype(ml_dtypes.bfloat16)


def signed(j):
    return np.where(j < MODES, j, j - 3 * MODES)


def build_tables():
    point = np.arange(GRID)
    angle = 2 * np.pi / GRID
    scale = 1.0 / math.sqrt(GRID**3)
    c = np.arange(MODES)
    weight = np.where(c == 0, 1.0, 2.0)
    cos_z = np.cos(angle * ((c[:, None] * point[None]) % GRID))
    sin_z = np.sin(angle * ((c[:, None] * point[None]) % GRID))
    b = np.arange(2 * MODES)
    turn = (signed(b)[:, None] * point[None]) % GRID
    cos_y, sin_y = np.cos(angle * turn), np.sin(angle * turn)
    re, im = slice(0, MODES), slice(MODES, HALF)

    za = np.zeros((GRID, 2 * LANES))
    za[:, 0:12], za[:, 12:24] = cos_z.T, -sin_z.T
    za[:, 128:140], za[:, 140:152] = -sin_z.T, -cos_z.T
    za *= scale

    order = (3 * np.arange(BETAS)[None, :] + np.arange(3)[:, None]).reshape(-1)
    ya = np.concatenate([cos_y[order], sin_y[order]], axis=1)

    first = np.zeros((320, 2 * LANES), ml_dtypes.bfloat16)
    first[0:128], first[128:256] = halves(za)
    first[256:280], first[288:312] = halves(ya)

    x_of = (2 * np.arange(64)[None, :] + np.arange(2)[:, None]).reshape(-1)
    xb = np.zeros((BETAS, 2 * OWNERS, GRID))
    for beta in range(BETAS):
        for slot in range(64):
            j = (beta - 3 * slot) % 8
            if j < 3:
                a = (3 * slot + j) // 8
                ang = angle * ((signed(np.array(a)) * x_of) % GRID)
                xb[beta, slot], xb[beta, 64 + slot] = np.cos(ang), np.sin(ang)
    xi = xb.transpose(0, 2, 1).copy()
    xp = xi.reshape(BETAS, 2, 64, 2 * OWNERS).transpose(0, 2, 1, 3).reshape(BETAS, GRID, 2 * OWNERS).copy()

    eb = np.zeros((2 * LANES, 3, 2, LANES))
    for bi in range(3):
        for ch in range(CH):
            for k in range(MODES):
                lr, li = bi * HALF + k, bi * HALF + MODES + k
                hr, hi = ch * HALF + k, ch * HALF + MODES + k
                for lane in (hr, hi):
                    eb[lr, bi, 0, lane] = 1
                    eb[LANES + li, bi, 0, lane] = 1
                sign = {hr: -1, hi: 1}
                for lane in (hr, hi):
                    eb[li, bi, 1, lane] = sign[lane]
                    eb[LANES + lr, bi, 1, lane] = -sign[lane]
    eb = eb.reshape(2 * LANES, 6 * LANES)

    zc = np.zeros((LANES, 2, GRID))
    for q in range(2):
        r, i = slice(q * HALF, q * HALF + MODES), slice(q * HALF + MODES, (q + 1) * HALF)
        rs, js = slice(PAIR + r.start, PAIR + r.stop), slice(PAIR + i.start, PAIR + i.stop)
        zc[r, q], zc[i, q] = weight[:, None] * cos_z, -weight[:, None] * sin_z
        zc[rs, q], zc[js, q] = -weight[:, None] * sin_z, -weight[:, None] * cos_z
    zh, zl = halves(zc.reshape(LANES, 2 * GRID) * scale)
    yh, yl = halves(np.concatenate([cos_y[order], sin_y[order]], axis=0))
    field = np.zeros((FIELD_ROWS, 2 * GRID), ml_dtypes.bfloat16)
    field[0:128], field[128:256], field[256:384] = zh, zh, zl
    field[384:640, :LANES], field[384:640, LANES:] = zh.T, zl.T
    field[640:688, :GRID], field[640:688, GRID:] = yh, yh
    field[688:736, :GRID] = yl
    field[736:864, 0:48], field[736:864, 48:96], field[736:864, 96:144] = yh.T, yl.T, yh.T

    ed = np.zeros((3, 2, LANES, 2, LANES))
    for bi in range(3):
        for ch in range(CH):
            for k in range(MODES):
                lr, li = bi * HALF + k, bi * HALF + MODES + k
                hr, hi = ch * HALF + k, ch * HALF + MODES + k
                ed[bi, 0, hr, 0, lr] = ed[bi, 0, hi, 0, lr] = 1
                ed[bi, 1, hr, 0, li], ed[bi, 1, hi, 0, li] = 1, -1
                ed[bi, 1, hr, 1, lr], ed[bi, 1, hi, 1, lr] = -1, 1
                ed[bi, 0, hr, 1, li] = ed[bi, 0, hi, 1, li] = 1
    ed = ed.reshape(6 * LANES, 2 * LANES)

    ze = np.zeros((LANES, 2, GRID))
    for q in range(2):
        at = q * PAIR
        ze[at : at + 12, q], ze[at + 12 : at + 24, q] = cos_z, -sin_z
        ze[at + 24 : at + 36, q], ze[at + 36 : at + 48, q] = -sin_z, -cos_z
    zh, zl = halves(ze.reshape(LANES, 2 * GRID) * scale)
    final = np.zeros((512, 2 * GRID), ml_dtypes.bfloat16)
    final[0:128], final[128:256], final[256:384] = zh, zh, zl
    final[384:512] = field[736:864]

    return dict(
        first=first, across=np.concatenate([h for t in (xi, xb, xp) for h in halves(t)], axis=1), field=field, final=final,
        eb=eb.astype(ml_dtypes.bfloat16), ed=ed.astype(ml_dtypes.bfloat16),
    )


def split(x):
    top = x.astype(BF16)
    return top, (x - top.astype(F32)).astype(BF16)


def dot(a, b):
    return lax.dot_general(a, b, (((1,), (0,)), ((), ())), preferred_element_type=F32)


def left(table_hi, table_lo, x):
    hi, lo = split(x)
    return dot(table_hi, hi) + dot(table_hi, lo) + dot(table_lo, hi)


def right(x, table_hi, table_lo):
    hi, lo = split(x)
    return dot(hi, table_hi) + dot(lo, table_hi) + dot(hi, table_lo)


def right_exact(x, table):
    hi, lo = split(x)
    return dot(hi, table) + dot(lo, table)


def part_mask(shape):
    lane = lax.broadcasted_iota(jnp.int32, shape, 1)
    return lax.rem(lane, HALF) < MODES


def swap(x, real):
    return jnp.where(real, pltpu.roll(x, LANES - MODES, 1), pltpu.roll(x, MODES, 1))


def first_kernel(
    pen_ref, rock_ref, well_ref, s_hbm, p_hbm, d_hbm, i_hbm, tab_hbm,
    out_ref, s_ref, p_ref, d_ref, i_ref, tab, t_ref, sems,
):
    pairs = (
        (tab_hbm, tab), (p_hbm, p_ref), (d_hbm, d_ref), (i_hbm, i_ref),
        (s_hbm, s_ref),
    )
    copies = [pltpu.make_async_copy(src, dst, sems.at[k]) for k, (src, dst) in enumerate(pairs)]
    for copy in copies:
        copy.start()
    for copy in copies[:-1]:
        copy.wait()
    x = jnp.concatenate([r[k] for r in (p_ref, d_ref, i_ref) for k in range(2)], axis=0)
    z = right(x, tab[0:128], tab[128:256])
    cols = [
        jnp.concatenate([z[k * GRID : (k + 1) * GRID, :LANES], z[k * GRID : (k + 1) * GRID, LANES:]], axis=0)
        for k in range(6)
    ]
    v = left(tab[256:280], tab[288:312], jnp.concatenate(cols, axis=1))
    lane = lax.broadcasted_iota(jnp.int32, (BETAS, LANES), 1)
    piece = [
        [v[8 * bi : 8 * bi + 8, k * LANES : (k + 1) * LANES] for bi in range(3)] for k in range(6)
    ]
    rows = [pltpu.roll(piece[k][2], 96, 1) for k in range(6)]
    for bi in range(2):
        for third in range(3):
            moved = pltpu.roll(piece[5][bi], 120 - 8 * third, 1)
            rows[3 * bi + third] = jnp.where(lane >= 120, moved, rows[3 * bi + third])
        total = piece[0][bi]
        for k in range(1, 5):
            total = total + pltpu.roll(piece[k][bi], HALF * k, 1)
        rows.append(total)
    for r in range(8):
        for kappa in range(KAPPAS):
            out_ref[kappa, :, r, :] = rows[r]

    copies[-1].wait()
    for part in range(2):
        rock = s_ref[part, 0] * rock_ref[0]
        well = s_ref[part, 0] * well_ref[0]
        for i in range(1, CHANNELS):
            x = s_ref[part, i]
            rock = rock + x * rock_ref[i]
            well = well + x * well_ref[i]
        t_ref[part, :, : rock.shape[1]] = rock
        t_ref[2 + part, :, : rock.shape[1]] = well
    lane = lax.broadcasted_iota(jnp.int32, (KAPPAS, LANES), 1)
    block = [[jnp.zeros((KAPPAS, LANES), F32) for _ in range(9)] for _ in range(2)]
    for ch in range(CH):
        for part in range(2):
            slot = 2 * ch + part
            inside = (lane >= slot * MODES) & (lane < (slot + 1) * MODES)
            for kind in range(2):
                x = t_ref[2 * kind + part, pl.ds(ch, KAPPAS, stride=CH), :]
                for row in range(9):
                    shift = ((slot - row) * MODES) % LANES
                    moved = pltpu.roll(x, shift, 1) if shift else x
                    block[kind][row] = jnp.where(inside, moved, block[kind][row])
    for j in range(3):
        beta = lax.rem(3 * pen_ref[0] + j, BETAS)
        for kind in range(2):
            for bi in range(3):
                r = 3 * kind + bi
                out_ref[:, beta, r, :] = out_ref[:, beta, r, :] + block[kind][3 * j + bi]


def owners_kernel(
    pen_ref, r_ref, across, eb, rock_ref, well_ref, mix_ref, off_ref, out_ref, scal_ref
):
    beta = lax.rem(pen_ref[0], BETAS)
    rock = mix_ref[0:1] * rock_ref[0]
    well = mix_ref[0:1] * well_ref[0]
    for i in range(1, CHANNELS):
        rock = rock + mix_ref[i : i + 1] * rock_ref[i]
        well = well + mix_ref[i : i + 1] * well_ref[i]
    scal_ref[0:1], scal_ref[1:2], scal_ref[2:3] = rock, well, off_ref[...]
    raw = [r_ref[:, r, :] for r in range(8)]
    lane = lax.broadcasted_iota(jnp.int32, (OWNERS, LANES), 1)

    def take(x, source, target, width, base):
        shift = (target - source) % LANES
        moved = pltpu.roll(x, shift, 1) if shift else x
        return jnp.where((lane >= target) & (lane < target + width), moved, base)

    planes = []
    for k in range(6):
        x = take(raw[k], 96, 48, HALF, jnp.zeros((OWNERS, LANES), F32))
        for bi in range(2):
            if k < 5:
                x = take(raw[6 + bi], HALF * k, HALF * bi, HALF, x)
            else:
                for third in range(3):
                    x = take(raw[3 * bi + third], 120, HALF * bi + 8 * third, 8, x)
        planes.append(x)
    fields = [jnp.concatenate(planes[2 * f : 2 * f + 2], axis=0) for f in range(3)]
    g = left(across[beta, 256:384], across[beta, 384:512], jnp.concatenate(fields, axis=1))
    pre = [
        right_exact(
            jnp.concatenate(
                [g[:64, f * LANES : (f + 1) * LANES], g[64:, f * LANES : (f + 1) * LANES]], axis=1
            ),
            eb[...],
        )
        for f in range(3)
    ]
    real = part_mask((OWNERS, LANES))
    stack = []
    for bi in range(3):
        t, w = raw[bi], raw[3 + bi]
        ts, ws = swap(t, real), swap(w, real)
        lo, mid, hi = 2 * bi * LANES, (2 * bi + 1) * LANES, (2 * bi + 2) * LANES
        coeff = (
            t * pre[0][:, lo:mid] + ts * pre[0][:, mid:hi]
            + w * pre[2][:, lo:mid] + ws * pre[2][:, mid:hi]
        )
        tangent = t * pre[1][:, lo:mid] + ts * pre[1][:, mid:hi]
        for q in (coeff, 0.25 * tangent):
            s = swap(q, real)
            stack.append(jnp.concatenate([q, jnp.where(real, -s, s)], axis=0))
    o = left(across[beta, 0:128], across[beta, 128:256], jnp.concatenate(stack, axis=1))
    for plane in range(2):
        piece = [o[plane * 64 : plane * 64 + 64, k * LANES : (k + 1) * LANES] for k in range(6)]
        for k in range(5):
            spare = take(piece[5], HALF * k, 96, HALF, piece[k]) if k < CH else piece[k]
            out_ref[:, plane, k * LANES : (k + 1) * LANES] = spare


ROOT = math.sqrt(2.0 / math.pi)
CUBIC = 0.044715


def twice_slope(x):
    square = x * x
    t = jnp.tanh(x * (ROOT + (ROOT * CUBIC) * square))
    return (1.0 + t) * (1.0 + (x * (ROOT + (3.0 * ROOT * CUBIC) * square)) * (1.0 - t))


def field_kernel(
    scal_hbm, r_ref, tab, p_ref, d_ref, i_ref,
    out_ref, local_ref, scal, z_ref, w0, w1, t0, t1, u0, u1, sem,
):
    copy = pltpu.make_async_copy(scal_hbm, scal, sem)
    copy.start()
    w_refs, t_refs, u_refs = (w0, w1), (t0, t1), (u0, u1)
    lane = lax.broadcasted_iota(jnp.int32, (HALF, LANES), 1)
    low, high = lane < PAIR, (lane >= PAIR) & (lane < 2 * PAIR)
    zero = jnp.zeros((HALF, LANES), F32)
    row = lax.broadcasted_iota(jnp.int32, (BETAS, LANES), 1)
    local_ref[...] = jnp.zeros_like(local_ref)

    def piece(kappa, plane, k):
        if k < 5:
            return r_ref[kappa, :, plane, k * LANES : (k + 1) * LANES]
        x = jnp.zeros((BETAS, LANES), F32)
        for q in range(CH):
            moved = pltpu.roll(r_ref[kappa, :, plane, q * LANES : (q + 1) * LANES], 32 + HALF * q, 1)
            x = jnp.where((row >= HALF * q) & (row < HALF * (q + 1)), moved, x)
        return x

    def front(k):
        kappas = [GROUP * k + m for m in range(GROUP)]
        w_ref = w_refs[k % 2]
        rhs = []
        for field in range(2):
            for plane in range(2):
                for kappa in kappas:
                    s = jnp.concatenate([piece(kappa, plane, bi * 2 + field) for bi in range(3)], axis=0)
                    right_pair = pltpu.roll(s, PAIR, 1)
                    left_pair = pltpu.roll(s, LANES - PAIR, 1)
                    rhs.append(
                        jnp.concatenate([jnp.where(low, s, zero), jnp.where(high, right_pair, zero)], axis=0)
                    )
                    rhs.append(
                        jnp.concatenate([jnp.where(low, left_pair, zero), jnp.where(high, s, zero)], axis=0)
                    )
        count = len(rhs)
        top, rest = split(jnp.concatenate(rhs, axis=1))
        y = dot(tab[736:864, :144], jnp.concatenate([top, top, rest], axis=0))
        top, rest = split(y)
        both = jnp.concatenate(
            [
                jnp.concatenate([h[:, c * LANES : (c + 1) * LANES] for h in (top, rest)], axis=1)
                for c in range(count)
            ],
            axis=0,
        )
        w_ref[...] = dot(both, tab[0:256]) + dot(both[:, :LANES], tab[256:384])

    def back(k):
        kappas = [GROUP * k + m for m in range(GROUP)]
        w_ref, t_ref, u_ref = w_refs[k % 2], t_refs[k % 2], u_refs[k % 2]
        half = 4 * GROUP * GRID
        at = 0
        for plane in range(2):
            perm, direc, inj = p_ref[plane], d_ref[plane], i_ref[plane]
            local = local_ref[plane]
            for kappa in kappas:
                for pair in range(2):
                    adj = []
                    for q in range(2):
                        o = kappa * CH + 2 * pair + q
                        rock = scal[0, o]
                        cells = slice(q * GRID, (q + 1) * GRID)
                        mixed = w_ref[at : at + GRID, cells] + rock * perm + scal[1, o] * inj + scal[2, o]
                        g = twice_slope(mixed)
                        a = g * g * (w_ref[half + at : half + at + GRID, cells] + (0.25 * rock) * direc)
                        local = local + rock * a
                        adj.append(a)
                    top, rest = split(jnp.concatenate(adj, axis=1))
                    t_ref[at : at + GRID], u_ref[at : at + GRID] = top, rest
                    at += GRID
            local_ref[plane] = local
        both = dot(t_ref[...], tab[384:640])
        z = both[:, :LANES] + both[:, LANES:] + dot(u_ref[...], tab[384:640, :LANES])
        top, rest = split(z)
        at = 0
        for plane in range(2):
            for kappa in kappas:
                for pair in range(2):
                    z_ref[4 * kappa + 2 * plane + pair, :GRID] = top[at : at + GRID]
                    z_ref[4 * kappa + 2 * plane + pair, GRID:] = rest[at : at + GRID]
                    at += GRID

    steps = KAPPAS // GROUP
    front(0)
    copy.wait()
    for k in range(steps):
        if k + 1 < steps:
            front(k + 1)
        back(k)

    for kappa in range(KAPPAS):
        v = dot(tab[640:736], jnp.concatenate([z_ref[4 * kappa + k] for k in range(4)], axis=1))
        v = v[:48] + v[48:]
        for plane in range(2):
            first, second = (v[:, k * LANES : (k + 1) * LANES] for k in (2 * plane, 2 * plane + 1))
            w = jnp.where(
                low,
                first[:HALF] + pltpu.roll(first[HALF:], LANES - PAIR, 1),
                jnp.where(high, pltpu.roll(second[:HALF], PAIR, 1) + second[HALF:], zero),
            )
            for bi in range(3):
                out_ref[kappa, :, plane, bi * LANES : (bi + 1) * LANES] = w[8 * bi : 8 * bi + 8]


GROUP = 1


def pull_kernel(pen_ref, r_ref, t_ref, across, ed, out_ref):
    beta = lax.rem(pen_ref[0], BETAS)
    fields = [
        jnp.concatenate([r_ref[:, k, bi * LANES : (bi + 1) * LANES] for k in range(2)], axis=0)
        for bi in range(3)
    ]
    g = left(across[beta, 256:384], across[beta, 384:512], jnp.concatenate(fields, axis=1))
    real = part_mask((OWNERS, LANES))
    parts = []
    for bi in range(3):
        t = t_ref[:, bi, :]
        fr, fi = g[:64, bi * LANES : (bi + 1) * LANES], g[64:, bi * LANES : (bi + 1) * LANES]
        s = swap(fi, real)
        v = fr + jnp.where(real, s, -s)
        parts += [t * v, t * swap(v, real)]
    q = right_exact(jnp.concatenate(parts, axis=1), ed[...])
    h = left(across[beta, 512:640], across[beta, 640:768], jnp.concatenate([q[:, :LANES], q[:, LANES:]], axis=0))
    for source in range(2):
        out_ref[GRID * source : GRID * source + GRID] = h


def final_kernel(r_ref, tab, mine_ref, theirs_ref, out_ref):
    lane = lax.broadcasted_iota(jnp.int32, (BETAS, LANES), 1)
    rows = [[], []]
    total = []
    for plane in range(2):
        x = r_ref[pl.ds(plane, BETAS, stride=2), :]
        for k in range(1, 2 * KAPPAS):
            x = x + r_ref[pl.ds(2 * BETAS * k + plane, BETAS, stride=2), :]
        total.append(x)
    for part in range(2):
        for bi in range(3):
            x = jnp.zeros((BETAS, LANES), F32)
            for plane in range(2):
                at = plane * PAIR + part * HALF
                shift = (at - HALF * bi) % LANES
                moved = pltpu.roll(total[plane], shift, 1) if shift else total[plane]
                x = jnp.where((lane >= at) & (lane < at + HALF), moved, x)
            rows[part].append(x)
    top, rest = split(jnp.concatenate(rows[0] + rows[1], axis=0))
    y = dot(tab[384:512, :144], jnp.concatenate([top, top, rest], axis=0))
    top, rest = split(y)
    z = dot(jnp.concatenate([top, rest], axis=1), tab[0:256]) + dot(top, tab[256:384])
    for plane in range(2):
        out_ref[plane] = z[:, plane * GRID : (plane + 1) * GRID] + (mine_ref[plane] + theirs_ref[plane])


VMEM = pl.BlockSpec(memory_space=pltpu.VMEM)
SMEM = pl.BlockSpec(memory_space=pltpu.SMEM)
HBM = pl.BlockSpec(memory_space=pltpu.HBM)
PARAMS = dict(compiler_params=pltpu.CompilerParams(vmem_limit_bytes=40 * 1024 * 1024))


def field_call(*operands):
    return pl.pallas_call(
        field_kernel,
        out_shape=[
            jax.ShapeDtypeStruct((KAPPAS, BETAS, 2, 3 * LANES), F32),
            jax.ShapeDtypeStruct((2, GRID, GRID), F32),
        ],
        in_specs=[HBM] + [VMEM] * 5,
        out_specs=[VMEM] * 2,
        scratch_shapes=[pltpu.SMEM((3, CHANNELS), F32)]
        + [
            pltpu.VMEM((4 * KAPPAS, 2 * GRID, LANES), BF16),
            *[pltpu.VMEM((8 * GROUP * GRID, 2 * GRID), F32)] * 2,
            *[pltpu.VMEM((4 * GROUP * GRID, 2 * GRID), BF16)] * 4,
            pltpu.SemaphoreType.DMA,
        ],
        name="field",
        **PARAMS,
    )(*operands)


def shards(permeability, direction, injection, lift_rock, lift_well, spectral, pointwise, offsets):
    tab = {
        k: tuple(jnp.asarray(x) for x in v) if isinstance(v, tuple) else jnp.asarray(v)
        for k, v in TABLES.items()
    }
    pen = lax.axis_index("pen").astype(jnp.int32).reshape(1)
    inj = injection[0]

    send = pl.pallas_call(
        first_kernel,
        out_shape=jax.ShapeDtypeStruct((KAPPAS, BETAS, 8, LANES), F32),
        in_specs=[SMEM] * 3 + [HBM] * 5,
        out_specs=VMEM,
        scratch_shapes=[
            pltpu.VMEM((2, CHANNELS, CHANNELS, spectral.shape[0]), F32),
            *[pltpu.VMEM((2, GRID, GRID), F32)] * 3,
            pltpu.VMEM((320, 2 * LANES), BF16),
            pltpu.VMEM((4, CHANNELS, LANES), F32),
            pltpu.SemaphoreType.DMA((5,)),
        ],
        name="first",
        compiler_params=pltpu.CompilerParams(vmem_limit_bytes=60 * 1024 * 1024),
    )(
        pen, lift_rock, lift_well, spectral.transpose(1, 2, 3, 0),
        permeability, direction, inj, tab["first"],
    )
    send = send.reshape(OWNERS, 8, LANES)
    owned = lax.all_to_all(send, "pen", 0, 0, tiled=True)

    send, scal = pl.pallas_call(
        owners_kernel,
        out_shape=[
            jax.ShapeDtypeStruct((OWNERS, 2, 5 * LANES), F32),
            jax.ShapeDtypeStruct((3, CHANNELS), F32),
        ],
        in_specs=[SMEM, VMEM, VMEM, VMEM, SMEM, SMEM, VMEM, VMEM],
        out_specs=[VMEM] * 2,
        name="owners",
        **PARAMS,
    )(
        pen, owned, tab["across"], tab["eb"],
        lift_rock, lift_well, pointwise, offsets.reshape(1, CHANNELS),
    )
    got = lax.all_to_all(send, "pen", 0, 0, tiled=True)

    send, local = field_call(scal, got.reshape(KAPPAS, BETAS, 2, 5 * LANES), tab["field"], permeability, direction, inj)
    theirs = lax.ppermute(local, "src", [(0, 1), (1, 0)])
    back = lax.all_to_all(send.reshape(OWNERS, 2, 3 * LANES), "pen", 0, 0, tiled=True)
    back, theirs = lax.optimization_barrier((back, theirs))

    send = pl.pallas_call(
        pull_kernel,
        out_shape=jax.ShapeDtypeStruct((4 * OWNERS, LANES), F32),
        in_specs=[SMEM] + [VMEM] * 4,
        out_specs=VMEM,
        name="pull",
        **PARAMS,
    )(pen, back, owned, tab["across"], tab["ed"])
    last = lax.all_to_all(send, ("src", "pen"), 0, 0, tiled=True)

    return pl.pallas_call(
        final_kernel,
        out_shape=jax.ShapeDtypeStruct((2, GRID, GRID), F32),
        in_specs=[VMEM] * 4,
        out_specs=VMEM,
        name="final",
        **PARAMS,
    )(last, tab["final"], local, theirs)


TABLES = build_tables()


def solution(mesh):
    placed = (
        P("pen", None, None),
        P("pen", None, None),
        P("src", "pen", None, None),
        P(),
        P(),
        P("pen", None, None, None),
        P(),
        P(),
    )
    return jax.shard_map(
        shards, mesh=mesh, in_specs=placed, out_specs=P("pen", None, None), check_vma=False
    )
```

```python
import math

import jax
import jax.numpy as jnp
import ml_dtypes
import numpy as np
from jax import lax
from jax.experimental import pallas as pl
from jax.experimental.pallas import tpu as pltpu
from jax.sharding import PartitionSpec as P

MODES = 12
GRID = 128
LANES = 128
BETAS = 8
KAPPAS = 8
OWNERS = BETAS * KAPPAS
CHANNELS = 32
CH = CHANNELS // KAPPAS
HALF = 24
PAIR = 48
FIELD_ROWS = 864
F32 = jnp.float32
BF16 = jnp.bfloat16


def halves(table):
    top = np.asarray(table, np.float32).astype(ml_dtypes.bfloat16)
    rest = (np.asarray(table, np.float64) - top.astype(np.float64)).astype(np.float32)
    return top, rest.astype(ml_dtypes.bfloat16)


def signed(j):
    return np.where(j < MODES, j, j - 3 * MODES)


def build_tables():
    point = np.arange(GRID)
    angle = 2 * np.pi / GRID
    scale = 1.0 / math.sqrt(GRID**3)
    c = np.arange(MODES)
    weight = np.where(c == 0, 1.0, 2.0)
    cos_z = np.cos(angle * ((c[:, None] * point[None]) % GRID))
    sin_z = np.sin(angle * ((c[:, None] * point[None]) % GRID))
    b = np.arange(2 * MODES)
    turn = (signed(b)[:, None] * point[None]) % GRID
    cos_y, sin_y = np.cos(angle * turn), np.sin(angle * turn)
    re, im = slice(0, MODES), slice(MODES, HALF)

    za = np.zeros((GRID, 2 * LANES))
    za[:, 0:12], za[:, 12:24] = cos_z.T, -sin_z.T
    za[:, 128:140], za[:, 140:152] = -sin_z.T, -cos_z.T
    za *= scale

    order = (3 * np.arange(BETAS)[None, :] + np.arange(3)[:, None]).reshape(-1)
    ya = np.concatenate([cos_y[order], sin_y[order]], axis=1)

    first = np.zeros((320, 2 * LANES), ml_dtypes.bfloat16)
    first[0:128], first[128:256] = halves(za)
    first[256:280], first[288:312] = halves(ya)

    x_of = (2 * np.arange(64)[None, :] + np.arange(2)[:, None]).reshape(-1)
    xb = np.zeros((BETAS, 2 * OWNERS, GRID))
    for beta in range(BETAS):
        for slot in range(64):
            j = (beta - 3 * slot) % 8
            if j < 3:
                a = (3 * slot + j) // 8
                ang = angle * ((signed(np.array(a)) * x_of) % GRID)
                xb[beta, slot], xb[beta, 64 + slot] = np.cos(ang), np.sin(ang)
    xi = xb.transpose(0, 2, 1).copy()
    xp = xi.reshape(BETAS, 2, 64, 2 * OWNERS).transpose(0, 2, 1, 3).reshape(BETAS, GRID, 2 * OWNERS).copy()

    eb = np.zeros((2 * LANES, 3, 2, LANES))
    for bi in range(3):
        for ch in range(CH):
            for k in range(MODES):
                lr, li = bi * HALF + k, bi * HALF + MODES + k
                hr, hi = ch * HALF + k, ch * HALF + MODES + k
                for lane in (hr, hi):
                    eb[lr, bi, 0, lane] = 1
                    eb[LANES + li, bi, 0, lane] = 1
                sign = {hr: -1, hi: 1}
                for lane in (hr, hi):
                    eb[li, bi, 1, lane] = sign[lane]
                    eb[LANES + lr, bi, 1, lane] = -sign[lane]
    eb = eb.reshape(2 * LANES, 6 * LANES)

    zc = np.zeros((LANES, 2, GRID))
    for q in range(2):
        r, i = slice(q * HALF, q * HALF + MODES), slice(q * HALF + MODES, (q + 1) * HALF)
        rs, js = slice(PAIR + r.start, PAIR + r.stop), slice(PAIR + i.start, PAIR + i.stop)
        zc[r, q], zc[i, q] = weight[:, None] * cos_z, -weight[:, None] * sin_z
        zc[rs, q], zc[js, q] = -weight[:, None] * sin_z, -weight[:, None] * cos_z
    zh, zl = halves(zc.reshape(LANES, 2 * GRID) * scale)
    yh, yl = halves(np.concatenate([cos_y[order], sin_y[order]], axis=0))
    field = np.zeros((FIELD_ROWS, 2 * GRID), ml_dtypes.bfloat16)
    field[0:128], field[128:256], field[256:384] = zh, zh, zl
    field[384:640, :LANES], field[384:640, LANES:] = zh.T, zl.T
    field[640:688, :GRID], field[640:688, GRID:] = yh, yh
    field[688:736, :GRID] = yl
    field[736:864, 0:48], field[736:864, 48:96], field[736:864, 96:144] = yh.T, yl.T, yh.T

    ed = np.zeros((3, 2, LANES, 2, LANES))
    for bi in range(3):
        for ch in range(CH):
            for k in range(MODES):
                lr, li = bi * HALF + k, bi * HALF + MODES + k
                hr, hi = ch * HALF + k, ch * HALF + MODES + k
                ed[bi, 0, hr, 0, lr] = ed[bi, 0, hi, 0, lr] = 1
                ed[bi, 1, hr, 0, li], ed[bi, 1, hi, 0, li] = 1, -1
                ed[bi, 1, hr, 1, lr], ed[bi, 1, hi, 1, lr] = -1, 1
                ed[bi, 0, hr, 1, li] = ed[bi, 0, hi, 1, li] = 1
    ed = ed.reshape(6 * LANES, 2 * LANES)

    ze = np.zeros((LANES, 2, GRID))
    for q in range(2):
        at = q * PAIR
        ze[at : at + 12, q], ze[at + 12 : at + 24, q] = cos_z, -sin_z
        ze[at + 24 : at + 36, q], ze[at + 36 : at + 48, q] = -sin_z, -cos_z
    zh, zl = halves(ze.reshape(LANES, 2 * GRID) * scale)
    final = np.zeros((512, 2 * GRID), ml_dtypes.bfloat16)
    final[0:128], final[128:256], final[256:384] = zh, zh, zl
    final[384:512] = field[736:864]

    return dict(
        first=first, across=np.concatenate([h for t in (xi, xb, xp) for h in halves(t)], axis=1), field=field, final=final,
        eb=eb.astype(ml_dtypes.bfloat16), ed=ed.astype(ml_dtypes.bfloat16),
    )


def split(x):
    top = x.astype(BF16)
    return top, (x - top.astype(F32)).astype(BF16)


def dot(a, b):
    return lax.dot_general(a, b, (((1,), (0,)), ((), ())), preferred_element_type=F32)


def left(table_hi, table_lo, x):
    hi, lo = split(x)
    return dot(table_hi, hi) + dot(table_hi, lo) + dot(table_lo, hi)


def right(x, table_hi, table_lo):
    hi, lo = split(x)
    return dot(hi, table_hi) + dot(lo, table_hi) + dot(hi, table_lo)


def right_exact(x, table):
    hi, lo = split(x)
    return dot(hi, table) + dot(lo, table)


def part_mask(shape):
    lane = lax.broadcasted_iota(jnp.int32, shape, 1)
    return lax.rem(lane, HALF) < MODES


def swap(x, real):
    return jnp.where(real, pltpu.roll(x, LANES - MODES, 1), pltpu.roll(x, MODES, 1))


def first_kernel(
    rock_hbm, well_hbm, s_hbm, p_hbm, d_hbm, i_hbm, tab_hbm,
    out_ref, rock_ref, well_ref, s_ref, p_ref, d_ref, i_ref, tab, t_ref, sems,
):
    pairs = (
        (tab_hbm, tab), (p_hbm, p_ref), (d_hbm, d_ref), (i_hbm, i_ref),
        (rock_hbm, rock_ref), (well_hbm, well_ref), (s_hbm, s_ref),
    )
    copies = [pltpu.make_async_copy(src, dst, sems.at[k]) for k, (src, dst) in enumerate(pairs)]
    for copy in copies:
        copy.start()
    for copy in copies[:-1]:
        copy.wait()
    x = jnp.concatenate([r[k] for r in (p_ref, d_ref, i_ref) for k in range(2)], axis=0)
    z = right(x, tab[0:128], tab[128:256])
    cols = [
        jnp.concatenate([z[k * GRID : (k + 1) * GRID, :LANES], z[k * GRID : (k + 1) * GRID, LANES:]], axis=0)
        for k in range(6)
    ]
    v = left(tab[256:280], tab[288:312], jnp.concatenate(cols, axis=1))
    lane = lax.broadcasted_iota(jnp.int32, (BETAS, LANES), 1)
    piece = [
        [v[8 * bi : 8 * bi + 8, k * LANES : (k + 1) * LANES] for bi in range(3)] for k in range(6)
    ]
    rows = [pltpu.roll(piece[k][2], 96, 1) for k in range(6)]
    for bi in range(2):
        for third in range(3):
            moved = pltpu.roll(piece[5][bi], 120 - 8 * third, 1)
            rows[3 * bi + third] = jnp.where(lane >= 120, moved, rows[3 * bi + third])
        total = piece[0][bi]
        for k in range(1, 5):
            total = total + pltpu.roll(piece[k][bi], HALF * k, 1)
        rows.append(total)
    for r in range(8):
        for kappa in range(KAPPAS):
            out_ref[kappa, :, r, :] = rows[r]

    copies[-1].wait()
    for part in range(2):
        rock = s_ref[part, 0] * rock_ref[0]
        well = s_ref[part, 0] * well_ref[0]
        for i in range(1, CHANNELS):
            x = s_ref[part, i]
            rock = rock + x * rock_ref[i]
            well = well + x * well_ref[i]
        t_ref[part, :, : rock.shape[1]] = rock
        t_ref[2 + part, :, : rock.shape[1]] = well
    lane = lax.broadcasted_iota(jnp.int32, (KAPPAS, LANES), 1)
    block = [[jnp.zeros((KAPPAS, LANES), F32) for _ in range(9)] for _ in range(2)]
    for ch in range(CH):
        for part in range(2):
            slot = 2 * ch + part
            inside = (lane >= slot * MODES) & (lane < (slot + 1) * MODES)
            for kind in range(2):
                x = t_ref[2 * kind + part, pl.ds(ch, KAPPAS, stride=CH), :]
                for row in range(9):
                    shift = ((slot - row) * MODES) % LANES
                    moved = pltpu.roll(x, shift, 1) if shift else x
                    block[kind][row] = jnp.where(inside, moved, block[kind][row])
    for j in range(3):
        beta = lax.rem(3 * lax.axis_index("pen") + j, BETAS)
        for kind in range(2):
            for bi in range(3):
                r = 3 * kind + bi
                out_ref[:, beta, r, :] = out_ref[:, beta, r, :] + block[kind][3 * j + bi]


def owners_kernel(
    r_ref, across, eb, rock_hbm, well_hbm, mix_ref, off_ref, out_ref, scal_ref, rock_ref, well_ref, sems
):
    beta = lax.rem(lax.axis_index("pen"), BETAS)
    copies = [
        pltpu.make_async_copy(src, dst, sems.at[k])
        for k, (src, dst) in enumerate(((rock_hbm, rock_ref), (well_hbm, well_ref)))
    ]
    for copy in copies:
        copy.start()
    raw = [r_ref[:, r, :] for r in range(8)]
    lane = lax.broadcasted_iota(jnp.int32, (OWNERS, LANES), 1)

    def take(x, source, target, width, base):
        shift = (target - source) % LANES
        moved = pltpu.roll(x, shift, 1) if shift else x
        return jnp.where((lane >= target) & (lane < target + width), moved, base)

    planes = []
    for k in range(6):
        x = take(raw[k], 96, 48, HALF, jnp.zeros((OWNERS, LANES), F32))
        for bi in range(2):
            if k < 5:
                x = take(raw[6 + bi], HALF * k, HALF * bi, HALF, x)
            else:
                for third in range(3):
                    x = take(raw[3 * bi + third], 120, HALF * bi + 8 * third, 8, x)
        planes.append(x)
    fields = [jnp.concatenate(planes[2 * f : 2 * f + 2], axis=0) for f in range(3)]
    g = left(across[beta, 256:384], across[beta, 384:512], jnp.concatenate(fields, axis=1))
    pre = [
        right_exact(
            jnp.concatenate(
                [g[:64, f * LANES : (f + 1) * LANES], g[64:, f * LANES : (f + 1) * LANES]], axis=1
            ),
            eb[...],
        )
        for f in range(3)
    ]
    real = part_mask((OWNERS, LANES))
    stack = []
    for bi in range(3):
        t, w = raw[bi], raw[3 + bi]
        ts, ws = swap(t, real), swap(w, real)
        lo, mid, hi = 2 * bi * LANES, (2 * bi + 1) * LANES, (2 * bi + 2) * LANES
        coeff = (
            t * pre[0][:, lo:mid] + ts * pre[0][:, mid:hi]
            + w * pre[2][:, lo:mid] + ws * pre[2][:, mid:hi]
        )
        tangent = t * pre[1][:, lo:mid] + ts * pre[1][:, mid:hi]
        for q in (coeff, 0.25 * tangent):
            s = swap(q, real)
            stack.append(jnp.concatenate([q, jnp.where(real, -s, s)], axis=0))
    o = left(across[beta, 0:128], across[beta, 128:256], jnp.concatenate(stack, axis=1))
    for plane in range(2):
        piece = [o[plane * 64 : plane * 64 + 64, k * LANES : (k + 1) * LANES] for k in range(6)]
        for k in range(5):
            spare = take(piece[5], HALF * k, 96, HALF, piece[k]) if k < CH else piece[k]
            out_ref[:, plane, k * LANES : (k + 1) * LANES] = spare
    for copy in copies:
        copy.wait()
    rock = mix_ref[0:1] * rock_ref[0]
    well = mix_ref[0:1] * well_ref[0]
    for i in range(1, CHANNELS):
        rock = rock + mix_ref[i : i + 1] * rock_ref[i]
        well = well + mix_ref[i : i + 1] * well_ref[i]
    scal_ref[0:1], scal_ref[1:2], scal_ref[2:3] = rock, well, off_ref[...]


ROOT = math.sqrt(2.0 / math.pi)
CUBIC = 0.044715


def twice_slope(x):
    square = x * x
    t = jnp.tanh(x * (ROOT + (ROOT * CUBIC) * square))
    return (1.0 + t) * (1.0 + (x * (ROOT + (3.0 * ROOT * CUBIC) * square)) * (1.0 - t))


def field_kernel(
    scal_hbm, r_ref, tab, p_ref, d_ref, i_ref,
    out_ref, local_ref, scal, z_ref, w0, w1, t0, t1, u0, u1, sem,
):
    copy = pltpu.make_async_copy(scal_hbm, scal, sem)
    copy.start()
    w_refs, t_refs, u_refs = (w0, w1), (t0, t1), (u0, u1)
    lane = lax.broadcasted_iota(jnp.int32, (HALF, LANES), 1)
    low, high = lane < PAIR, (lane >= PAIR) & (lane < 2 * PAIR)
    zero = jnp.zeros((HALF, LANES), F32)
    row = lax.broadcasted_iota(jnp.int32, (BETAS, LANES), 1)
    local_ref[...] = jnp.zeros_like(local_ref)

    def piece(kappa, plane, k):
        if k < 5:
            return r_ref[kappa, :, plane, k * LANES : (k + 1) * LANES]
        x = jnp.zeros((BETAS, LANES), F32)
        for q in range(CH):
            moved = pltpu.roll(r_ref[kappa, :, plane, q * LANES : (q + 1) * LANES], 32 + HALF * q, 1)
            x = jnp.where((row >= HALF * q) & (row < HALF * (q + 1)), moved, x)
        return x

    def front(k):
        kappas = [GROUP * k + m for m in range(GROUP)]
        w_ref = w_refs[k % 2]
        rhs = []
        for field in range(2):
            for plane in range(2):
                for kappa in kappas:
                    s = jnp.concatenate([piece(kappa, plane, bi * 2 + field) for bi in range(3)], axis=0)
                    right_pair = pltpu.roll(s, PAIR, 1)
                    left_pair = pltpu.roll(s, LANES - PAIR, 1)
                    rhs.append(
                        jnp.concatenate([jnp.where(low, s, zero), jnp.where(high, right_pair, zero)], axis=0)
                    )
                    rhs.append(
                        jnp.concatenate([jnp.where(low, left_pair, zero), jnp.where(high, s, zero)], axis=0)
                    )
        count = len(rhs)
        top, rest = split(jnp.concatenate(rhs, axis=1))
        y = dot(tab[736:864, :144], jnp.concatenate([top, top, rest], axis=0))
        top, rest = split(y)
        both = jnp.concatenate(
            [
                jnp.concatenate([h[:, c * LANES : (c + 1) * LANES] for h in (top, rest)], axis=1)
                for c in range(count)
            ],
            axis=0,
        )
        w_ref[...] = dot(both, tab[0:256]) + dot(both[:, :LANES], tab[256:384])

    def back(k):
        kappas = [GROUP * k + m for m in range(GROUP)]
        w_ref, t_ref, u_ref = w_refs[k % 2], t_refs[k % 2], u_refs[k % 2]
        half = 4 * GROUP * GRID
        at = 0
        for plane in range(2):
            perm, direc, inj = p_ref[plane], d_ref[plane], i_ref[plane]
            local = local_ref[plane]
            for kappa in kappas:
                for pair in range(2):
                    adj = []
                    for q in range(2):
                        o = kappa * CH + 2 * pair + q
                        rock = scal[0, o]
                        cells = slice(q * GRID, (q + 1) * GRID)
                        mixed = w_ref[at : at + GRID, cells] + rock * perm + scal[1, o] * inj + scal[2, o]
                        g = twice_slope(mixed)
                        a = g * g * (w_ref[half + at : half + at + GRID, cells] + (0.25 * rock) * direc)
                        local = local + rock * a
                        adj.append(a)
                    top, rest = split(jnp.concatenate(adj, axis=1))
                    t_ref[at : at + GRID], u_ref[at : at + GRID] = top, rest
                    at += GRID
            local_ref[plane] = local
        both = dot(t_ref[...], tab[384:640])
        z = both[:, :LANES] + both[:, LANES:] + dot(u_ref[...], tab[384:640, :LANES])
        top, rest = split(z)
        at = 0
        for plane in range(2):
            for kappa in kappas:
                for pair in range(2):
                    z_ref[4 * kappa + 2 * plane + pair, :GRID] = top[at : at + GRID]
                    z_ref[4 * kappa + 2 * plane + pair, GRID:] = rest[at : at + GRID]
                    at += GRID

    steps = KAPPAS // GROUP
    front(0)
    copy.wait()
    for k in range(steps):
        if k + 1 < steps:
            front(k + 1)
        back(k)

    for kappa in range(KAPPAS):
        v = dot(tab[640:736], jnp.concatenate([z_ref[4 * kappa + k] for k in range(4)], axis=1))
        v = v[:48] + v[48:]
        for plane in range(2):
            first, second = (v[:, k * LANES : (k + 1) * LANES] for k in (2 * plane, 2 * plane + 1))
            w = jnp.where(
                low,
                first[:HALF] + pltpu.roll(first[HALF:], LANES - PAIR, 1),
                jnp.where(high, pltpu.roll(second[:HALF], PAIR, 1) + second[HALF:], zero),
            )
            for bi in range(3):
                out_ref[kappa, :, plane, bi * LANES : (bi + 1) * LANES] = w[8 * bi : 8 * bi + 8]


GROUP = 1


def pull_kernel(r_ref, t_ref, across, ed, out_ref):
    beta = lax.rem(lax.axis_index("pen"), BETAS)
    fields = [
        jnp.concatenate([r_ref[:, k, bi * LANES : (bi + 1) * LANES] for k in range(2)], axis=0)
        for bi in range(3)
    ]
    g = left(across[beta, 256:384], across[beta, 384:512], jnp.concatenate(fields, axis=1))
    real = part_mask((OWNERS, LANES))
    parts = []
    for bi in range(3):
        t = t_ref[:, bi, :]
        fr, fi = g[:64, bi * LANES : (bi + 1) * LANES], g[64:, bi * LANES : (bi + 1) * LANES]
        s = swap(fi, real)
        v = fr + jnp.where(real, s, -s)
        parts += [t * v, t * swap(v, real)]
    q = right_exact(jnp.concatenate(parts, axis=1), ed[...])
    h = left(across[beta, 512:640], across[beta, 640:768], jnp.concatenate([q[:, :LANES], q[:, LANES:]], axis=0))
    for source in range(2):
        out_ref[GRID * source : GRID * source + GRID] = h


def final_kernel(r_ref, tab, mine_ref, theirs_ref, out_ref):
    lane = lax.broadcasted_iota(jnp.int32, (BETAS, LANES), 1)
    rows = [[], []]
    total = []
    for plane in range(2):
        x = r_ref[pl.ds(plane, BETAS, stride=2), :]
        for k in range(1, 2 * KAPPAS):
            x = x + r_ref[pl.ds(2 * BETAS * k + plane, BETAS, stride=2), :]
        total.append(x)
    for part in range(2):
        for bi in range(3):
            x = jnp.zeros((BETAS, LANES), F32)
            for plane in range(2):
                at = plane * PAIR + part * HALF
                shift = (at - HALF * bi) % LANES
                moved = pltpu.roll(total[plane], shift, 1) if shift else total[plane]
                x = jnp.where((lane >= at) & (lane < at + HALF), moved, x)
            rows[part].append(x)
    top, rest = split(jnp.concatenate(rows[0] + rows[1], axis=0))
    y = dot(tab[384:512, :144], jnp.concatenate([top, top, rest], axis=0))
    top, rest = split(y)
    z = dot(jnp.concatenate([top, rest], axis=1), tab[0:256]) + dot(top, tab[256:384])
    for plane in range(2):
        out_ref[plane] = z[:, plane * GRID : (plane + 1) * GRID] + (mine_ref[plane] + theirs_ref[plane])


VMEM = pl.BlockSpec(memory_space=pltpu.VMEM)
SMEM = pl.BlockSpec(memory_space=pltpu.SMEM)
HBM = pl.BlockSpec(memory_space=pltpu.HBM)
PARAMS = dict(compiler_params=pltpu.CompilerParams(vmem_limit_bytes=40 * 1024 * 1024))


def field_call(*operands):
    return pl.pallas_call(
        field_kernel,
        out_shape=[
            jax.ShapeDtypeStruct((KAPPAS, BETAS, 2, 3 * LANES), F32),
            jax.ShapeDtypeStruct((2, GRID, GRID), F32),
        ],
        in_specs=[HBM] + [VMEM] * 5,
        out_specs=[VMEM] * 2,
        scratch_shapes=[pltpu.SMEM((3, CHANNELS), F32)]
        + [
            pltpu.VMEM((4 * KAPPAS, 2 * GRID, LANES), BF16),
            *[pltpu.VMEM((8 * GROUP * GRID, 2 * GRID), F32)] * 2,
            *[pltpu.VMEM((4 * GROUP * GRID, 2 * GRID), BF16)] * 4,
            pltpu.SemaphoreType.DMA,
        ],
        name="field",
        **PARAMS,
    )(*operands)


def shards(permeability, direction, injection, lift_rock, lift_well, spectral, pointwise, offsets):
    tab = {
        k: tuple(jnp.asarray(x) for x in v) if isinstance(v, tuple) else jnp.asarray(v)
        for k, v in TABLES.items()
    }
    inj = injection[0]

    send = pl.pallas_call(
        first_kernel,
        out_shape=jax.ShapeDtypeStruct((KAPPAS, BETAS, 8, LANES), F32),
        in_specs=[HBM] * 7,
        out_specs=VMEM,
        scratch_shapes=[
            *[pltpu.SMEM((CHANNELS,), F32)] * 2,
            pltpu.VMEM((2, CHANNELS, CHANNELS, spectral.shape[0]), F32),
            *[pltpu.VMEM((2, GRID, GRID), F32)] * 3,
            pltpu.VMEM((320, 2 * LANES), BF16),
            pltpu.VMEM((4, CHANNELS, LANES), F32),
            pltpu.SemaphoreType.DMA((7,)),
        ],
        name="first",
        compiler_params=pltpu.CompilerParams(vmem_limit_bytes=60 * 1024 * 1024),
    )(
        lift_rock, lift_well, spectral.transpose(1, 2, 3, 0),
        permeability, direction, inj, tab["first"],
    )
    send = send.reshape(OWNERS, 8, LANES)
    owned = lax.all_to_all(send, "pen", 0, 0, tiled=True)

    send, scal = pl.pallas_call(
        owners_kernel,
        out_shape=[
            jax.ShapeDtypeStruct((OWNERS, 2, 5 * LANES), F32),
            jax.ShapeDtypeStruct((3, CHANNELS), F32),
        ],
        in_specs=[VMEM, VMEM, VMEM, HBM, HBM, VMEM, VMEM],
        out_specs=[VMEM] * 2,
        scratch_shapes=[pltpu.SMEM((CHANNELS,), F32)] * 2 + [pltpu.SemaphoreType.DMA((2,))],
        name="owners",
        **PARAMS,
    )(
        owned, tab["across"], tab["eb"],
        lift_rock, lift_well, pointwise, offsets.reshape(1, CHANNELS),
    )
    got = lax.all_to_all(send, "pen", 0, 0, tiled=True)

    send, local = field_call(scal, got.reshape(KAPPAS, BETAS, 2, 5 * LANES), tab["field"], permeability, direction, inj)
    theirs = lax.ppermute(local, "src", [(0, 1), (1, 0)])
    back = lax.all_to_all(send.reshape(OWNERS, 2, 3 * LANES), "pen", 0, 0, tiled=True)

    send = pl.pallas_call(
        pull_kernel,
        out_shape=jax.ShapeDtypeStruct((4 * OWNERS, LANES), F32),
        in_specs=[VMEM] * 4,
        out_specs=VMEM,
        name="pull",
        **PARAMS,
    )(back, owned, tab["across"], tab["ed"])
    last = lax.all_to_all(send, ("src", "pen"), 0, 0, tiled=True)

    return pl.pallas_call(
        final_kernel,
        out_shape=jax.ShapeDtypeStruct((2, GRID, GRID), F32),
        in_specs=[VMEM] * 4,
        out_specs=VMEM,
        name="final",
        **PARAMS,
    )(last, tab["final"], local, theirs)


TABLES = build_tables()


def solution(mesh):
    placed = (
        P("pen", None, None),
        P("pen", None, None),
        P("src", "pen", None, None),
        P(),
        P(),
        P("pen", None, None, None),
        P(),
        P(),
    )
    return jax.shard_map(
        shards, mesh=mesh, in_specs=placed, out_specs=P("pen", None, None), check_vma=False
    )
```

```python
import math

import jax
import jax.numpy as jnp
import ml_dtypes
import numpy as np
from jax import lax
from jax.experimental import pallas as pl
from jax.experimental.pallas import tpu as pltpu
from jax.sharding import PartitionSpec as P

MODES = 12
GRID = 128
LANES = 128
BETAS = 8
KAPPAS = 8
OWNERS = BETAS * KAPPAS
CHANNELS = 32
CH = CHANNELS // KAPPAS
HALF = 24
PAIR = 48
FIELD_ROWS = 864
F32 = jnp.float32
BF16 = jnp.bfloat16


def halves(table):
    top = np.asarray(table, np.float32).astype(ml_dtypes.bfloat16)
    rest = (np.asarray(table, np.float64) - top.astype(np.float64)).astype(np.float32)
    return top, rest.astype(ml_dtypes.bfloat16)


def signed(j):
    return np.where(j < MODES, j, j - 3 * MODES)


def build_tables():
    point = np.arange(GRID)
    angle = 2 * np.pi / GRID
    scale = 1.0 / math.sqrt(GRID**3)
    c = np.arange(MODES)
    weight = np.where(c == 0, 1.0, 2.0)
    cos_z = np.cos(angle * ((c[:, None] * point[None]) % GRID))
    sin_z = np.sin(angle * ((c[:, None] * point[None]) % GRID))
    b = np.arange(2 * MODES)
    turn = (signed(b)[:, None] * point[None]) % GRID
    cos_y, sin_y = np.cos(angle * turn), np.sin(angle * turn)
    re, im = slice(0, MODES), slice(MODES, HALF)

    za = np.zeros((GRID, 2 * LANES))
    za[:, 0:12], za[:, 12:24] = cos_z.T, -sin_z.T
    za[:, 128:140], za[:, 140:152] = -sin_z.T, -cos_z.T
    za *= scale

    order = (3 * np.arange(BETAS)[None, :] + np.arange(3)[:, None]).reshape(-1)
    ya = np.concatenate([cos_y[order], sin_y[order]], axis=1)

    first = np.zeros((320, 2 * LANES), ml_dtypes.bfloat16)
    first[0:128], first[128:256] = halves(za)
    first[256:280], first[288:312] = halves(ya)

    x_of = (2 * np.arange(64)[None, :] + np.arange(2)[:, None]).reshape(-1)
    xb = np.zeros((BETAS, 2 * OWNERS, GRID))
    for beta in range(BETAS):
        for slot in range(64):
            j = (beta - 3 * slot) % 8
            if j < 3:
                a = (3 * slot + j) // 8
                ang = angle * ((signed(np.array(a)) * x_of) % GRID)
                xb[beta, slot], xb[beta, 64 + slot] = np.cos(ang), np.sin(ang)
    xi = xb.transpose(0, 2, 1).copy()
    xp = xi.reshape(BETAS, 2, 64, 2 * OWNERS).transpose(0, 2, 1, 3).reshape(BETAS, GRID, 2 * OWNERS).copy()

    eb = np.zeros((2 * LANES, 3, 2, LANES))
    for bi in range(3):
        for ch in range(CH):
            for k in range(MODES):
                lr, li = bi * HALF + k, bi * HALF + MODES + k
                hr, hi = ch * HALF + k, ch * HALF + MODES + k
                for lane in (hr, hi):
                    eb[lr, bi, 0, lane] = 1
                    eb[LANES + li, bi, 0, lane] = 1
                sign = {hr: -1, hi: 1}
                for lane in (hr, hi):
                    eb[li, bi, 1, lane] = sign[lane]
                    eb[LANES + lr, bi, 1, lane] = -sign[lane]
    eb = eb.reshape(2 * LANES, 6 * LANES)

    zc = np.zeros((LANES, 2, GRID))
    for q in range(2):
        r, i = slice(q * HALF, q * HALF + MODES), slice(q * HALF + MODES, (q + 1) * HALF)
        rs, js = slice(PAIR + r.start, PAIR + r.stop), slice(PAIR + i.start, PAIR + i.stop)
        zc[r, q], zc[i, q] = weight[:, None] * cos_z, -weight[:, None] * sin_z
        zc[rs, q], zc[js, q] = -weight[:, None] * sin_z, -weight[:, None] * cos_z
    zh, zl = halves(zc.reshape(LANES, 2 * GRID) * scale)
    yh, yl = halves(np.concatenate([cos_y[order], sin_y[order]], axis=0))
    field = np.zeros((FIELD_ROWS, 2 * GRID), ml_dtypes.bfloat16)
    field[0:128], field[128:256], field[256:384] = zh, zh, zl
    field[384:640, :LANES], field[384:640, LANES:] = zh.T, zl.T
    field[640:688, :GRID], field[640:688, GRID:] = yh, yh
    field[688:736, :GRID] = yl
    field[736:864, 0:48], field[736:864, 48:96], field[736:864, 96:144] = yh.T, yl.T, yh.T

    ed = np.zeros((3, 2, LANES, 2, LANES))
    for bi in range(3):
        for ch in range(CH):
            for k in range(MODES):
                lr, li = bi * HALF + k, bi * HALF + MODES + k
                hr, hi = ch * HALF + k, ch * HALF + MODES + k
                ed[bi, 0, hr, 0, lr] = ed[bi, 0, hi, 0, lr] = 1
                ed[bi, 1, hr, 0, li], ed[bi, 1, hi, 0, li] = 1, -1
                ed[bi, 1, hr, 1, lr], ed[bi, 1, hi, 1, lr] = -1, 1
                ed[bi, 0, hr, 1, li] = ed[bi, 0, hi, 1, li] = 1
    ed = ed.reshape(6 * LANES, 2 * LANES)

    ze = np.zeros((LANES, 2, GRID))
    for q in range(2):
        at = q * PAIR
        ze[at : at + 12, q], ze[at + 12 : at + 24, q] = cos_z, -sin_z
        ze[at + 24 : at + 36, q], ze[at + 36 : at + 48, q] = -sin_z, -cos_z
    zh, zl = halves(ze.reshape(LANES, 2 * GRID) * scale)
    final = np.zeros((512, 2 * GRID), ml_dtypes.bfloat16)
    final[0:128], final[128:256], final[256:384] = zh, zh, zl
    final[384:512] = field[736:864]

    return dict(
        first=first, across=np.concatenate([h for t in (xi, xb, xp) for h in halves(t)], axis=1), field=field, final=final,
        eb=eb.astype(ml_dtypes.bfloat16), ed=ed.astype(ml_dtypes.bfloat16),
    )


def split(x):
    top = x.astype(BF16)
    return top, (x - top.astype(F32)).astype(BF16)


def dot(a, b):
    return lax.dot_general(a, b, (((1,), (0,)), ((), ())), preferred_element_type=F32)


def left(table_hi, table_lo, x):
    hi, lo = split(x)
    return dot(table_hi, hi) + dot(table_hi, lo) + dot(table_lo, hi)


def right(x, table_hi, table_lo):
    hi, lo = split(x)
    return dot(hi, table_hi) + dot(lo, table_hi) + dot(hi, table_lo)


def right_exact(x, table):
    hi, lo = split(x)
    return dot(hi, table) + dot(lo, table)


def part_mask(shape):
    lane = lax.broadcasted_iota(jnp.int32, shape, 1)
    return lax.rem(lane, HALF) < MODES


def swap(x, real):
    return jnp.where(real, pltpu.roll(x, LANES - MODES, 1), pltpu.roll(x, MODES, 1))


def first_kernel(
    rock_hbm, well_hbm, s_hbm, p_hbm, d_hbm, i_hbm, tab_hbm,
    out_ref, rock_ref, well_ref, s_ref, p_ref, d_ref, i_ref, tab, t_ref, sems,
):
    pairs = (
        (tab_hbm, tab), (p_hbm, p_ref), (d_hbm, d_ref), (i_hbm, i_ref),
        (rock_hbm, rock_ref), (well_hbm, well_ref), (s_hbm, s_ref),
    )
    copies = [pltpu.make_async_copy(src, dst, sems.at[k]) for k, (src, dst) in enumerate(pairs)]
    for copy in copies:
        copy.start()
    for copy in copies[:-1]:
        copy.wait()
    x = jnp.concatenate([r[k] for r in (p_ref, d_ref, i_ref) for k in range(2)], axis=0)
    z = right(x, tab[0:128], tab[128:256])
    cols = [
        jnp.concatenate([z[k * GRID : (k + 1) * GRID, :LANES], z[k * GRID : (k + 1) * GRID, LANES:]], axis=0)
        for k in range(6)
    ]
    v = left(tab[256:280], tab[288:312], jnp.concatenate(cols, axis=1))
    lane = lax.broadcasted_iota(jnp.int32, (BETAS, LANES), 1)
    piece = [
        [v[8 * bi : 8 * bi + 8, k * LANES : (k + 1) * LANES] for bi in range(3)] for k in range(6)
    ]
    rows = [pltpu.roll(piece[k][2], 96, 1) for k in range(6)]
    for bi in range(2):
        for third in range(3):
            moved = pltpu.roll(piece[5][bi], 120 - 8 * third, 1)
            rows[3 * bi + third] = jnp.where(lane >= 120, moved, rows[3 * bi + third])
        total = piece[0][bi]
        for k in range(1, 5):
            total = total + pltpu.roll(piece[k][bi], HALF * k, 1)
        rows.append(total)
    for r in range(8):
        for kappa in range(KAPPAS):
            out_ref[kappa, :, r, :] = rows[r]

    copies[-1].wait()
    for part in range(2):
        rock = s_ref[part, 0] * rock_ref[0]
        well = s_ref[part, 0] * well_ref[0]
        for i in range(1, CHANNELS):
            x = s_ref[part, i]
            rock = rock + x * rock_ref[i]
            well = well + x * well_ref[i]
        t_ref[part, :, : rock.shape[1]] = rock
        t_ref[2 + part, :, : rock.shape[1]] = well
    lane = lax.broadcasted_iota(jnp.int32, (KAPPAS, LANES), 1)
    block = [[jnp.zeros((KAPPAS, LANES), F32) for _ in range(9)] for _ in range(2)]
    for ch in range(CH):
        for part in range(2):
            slot = 2 * ch + part
            inside = (lane >= slot * MODES) & (lane < (slot + 1) * MODES)
            for kind in range(2):
                x = t_ref[2 * kind + part, pl.ds(ch, KAPPAS, stride=CH), :]
                for row in range(9):
                    shift = ((slot - row) * MODES) % LANES
                    moved = pltpu.roll(x, shift, 1) if shift else x
                    block[kind][row] = jnp.where(inside, moved, block[kind][row])
    for j in range(3):
        beta = lax.rem(3 * lax.axis_index("pen") + j, BETAS)
        for kind in range(2):
            for bi in range(3):
                r = 3 * kind + bi
                out_ref[:, beta, r, :] = out_ref[:, beta, r, :] + block[kind][3 * j + bi]


def owners_kernel(
    r_ref, across, eb, rock_hbm, well_hbm, mix_ref, off_ref, out_ref, scal_ref, rock_ref, well_ref, sems
):
    beta = lax.rem(lax.axis_index("pen"), BETAS)
    copies = [
        pltpu.make_async_copy(src, dst, sems.at[k])
        for k, (src, dst) in enumerate(((rock_hbm, rock_ref), (well_hbm, well_ref)))
    ]
    for copy in copies:
        copy.start()
    raw = [r_ref[:, r, :] for r in range(8)]
    lane = lax.broadcasted_iota(jnp.int32, (OWNERS, LANES), 1)

    def take(x, source, target, width, base):
        shift = (target - source) % LANES
        moved = pltpu.roll(x, shift, 1) if shift else x
        return jnp.where((lane >= target) & (lane < target + width), moved, base)

    planes = []
    for k in range(6):
        x = take(raw[k], 96, 48, HALF, jnp.zeros((OWNERS, LANES), F32))
        for bi in range(2):
            if k < 5:
                x = take(raw[6 + bi], HALF * k, HALF * bi, HALF, x)
            else:
                for third in range(3):
                    x = take(raw[3 * bi + third], 120, HALF * bi + 8 * third, 8, x)
        planes.append(x)
    fields = [jnp.concatenate(planes[2 * f : 2 * f + 2], axis=0) for f in range(3)]
    g = left(across[beta, 256:384], across[beta, 384:512], jnp.concatenate(fields, axis=1))
    wide = jnp.concatenate(
        [
            jnp.concatenate([g[k : k + 64, f * LANES : (f + 1) * LANES] for k in (0, 64)], axis=1)
            for f in range(3)
        ],
        axis=0,
    )
    wide = right_exact(wide, eb[...])
    pre = [wide[OWNERS * f : OWNERS * (f + 1)] for f in range(3)]
    real = part_mask((OWNERS, LANES))
    stack = []
    for bi in range(3):
        t, w = raw[bi], raw[3 + bi]
        ts, ws = swap(t, real), swap(w, real)
        lo, mid, hi = 2 * bi * LANES, (2 * bi + 1) * LANES, (2 * bi + 2) * LANES
        coeff = (
            t * pre[0][:, lo:mid] + ts * pre[0][:, mid:hi]
            + w * pre[2][:, lo:mid] + ws * pre[2][:, mid:hi]
        )
        tangent = t * pre[1][:, lo:mid] + ts * pre[1][:, mid:hi]
        for q in (coeff, 0.25 * tangent):
            s = swap(q, real)
            stack.append(jnp.concatenate([q, jnp.where(real, -s, s)], axis=0))
    o = left(across[beta, 0:128], across[beta, 128:256], jnp.concatenate(stack, axis=1))
    for plane in range(2):
        piece = [o[plane * 64 : plane * 64 + 64, k * LANES : (k + 1) * LANES] for k in range(6)]
        for k in range(5):
            spare = take(piece[5], HALF * k, 96, HALF, piece[k]) if k < CH else piece[k]
            out_ref[:, plane, k * LANES : (k + 1) * LANES] = spare
    for copy in copies:
        copy.wait()
    rock = mix_ref[0:1] * rock_ref[0]
    well = mix_ref[0:1] * well_ref[0]
    for i in range(1, CHANNELS):
        rock = rock + mix_ref[i : i + 1] * rock_ref[i]
        well = well + mix_ref[i : i + 1] * well_ref[i]
    scal_ref[0:1], scal_ref[1:2], scal_ref[2:3] = rock, well, off_ref[...]


ROOT = math.sqrt(2.0 / math.pi)
CUBIC = 0.044715


def twice_slope(x):
    square = x * x
    t = jnp.tanh(x * (ROOT + (ROOT * CUBIC) * square))
    return (1.0 + t) * (1.0 + (x * (ROOT + (3.0 * ROOT * CUBIC) * square)) * (1.0 - t))


def field_kernel(
    scal_hbm, r_ref, tab, p_ref, d_ref, i_ref,
    out_ref, local_ref, scal, z_ref, w0, w1, t0, t1, u0, u1, sem,
):
    copy = pltpu.make_async_copy(scal_hbm, scal, sem)
    copy.start()
    w_refs, t_refs, u_refs = (w0, w1), (t0, t1), (u0, u1)
    lane = lax.broadcasted_iota(jnp.int32, (HALF, LANES), 1)
    low, high = lane < PAIR, (lane >= PAIR) & (lane < 2 * PAIR)
    zero = jnp.zeros((HALF, LANES), F32)
    row = lax.broadcasted_iota(jnp.int32, (BETAS, LANES), 1)
    local_ref[...] = jnp.zeros_like(local_ref)

    def piece(kappa, plane, k):
        if k < 5:
            return r_ref[kappa, :, plane, k * LANES : (k + 1) * LANES]
        x = jnp.zeros((BETAS, LANES), F32)
        for q in range(CH):
            moved = pltpu.roll(r_ref[kappa, :, plane, q * LANES : (q + 1) * LANES], 32 + HALF * q, 1)
            x = jnp.where((row >= HALF * q) & (row < HALF * (q + 1)), moved, x)
        return x

    def front(k):
        kappas = [GROUP * k + m for m in range(GROUP)]
        w_ref = w_refs[k % 2]
        rhs = []
        for field in range(2):
            for plane in range(2):
                for kappa in kappas:
                    s = jnp.concatenate([piece(kappa, plane, bi * 2 + field) for bi in range(3)], axis=0)
                    right_pair = pltpu.roll(s, PAIR, 1)
                    left_pair = pltpu.roll(s, LANES - PAIR, 1)
                    rhs.append(
                        jnp.concatenate([jnp.where(low, s, zero), jnp.where(high, right_pair, zero)], axis=0)
                    )
                    rhs.append(
                        jnp.concatenate([jnp.where(low, left_pair, zero), jnp.where(high, s, zero)], axis=0)
                    )
        count = len(rhs)
        top, rest = split(jnp.concatenate(rhs, axis=1))
        y = dot(tab[736:864, :144], jnp.concatenate([top, top, rest], axis=0))
        top, rest = split(y)
        both = jnp.concatenate(
            [
                jnp.concatenate([h[:, c * LANES : (c + 1) * LANES] for h in (top, rest)], axis=1)
                for c in range(count)
            ],
            axis=0,
        )
        w_ref[...] = dot(both, tab[0:256]) + dot(both[:, :LANES], tab[256:384])

    def back(k):
        kappas = [GROUP * k + m for m in range(GROUP)]
        w_ref, t_ref, u_ref = w_refs[k % 2], t_refs[k % 2], u_refs[k % 2]
        half = 4 * GROUP * GRID
        at = 0
        for plane in range(2):
            perm, direc, inj = p_ref[plane], d_ref[plane], i_ref[plane]
            local = local_ref[plane]
            for kappa in kappas:
                for pair in range(2):
                    adj = []
                    for q in range(2):
                        o = kappa * CH + 2 * pair + q
                        rock = scal[0, o]
                        cells = slice(q * GRID, (q + 1) * GRID)
                        mixed = w_ref[at : at + GRID, cells] + rock * perm + scal[1, o] * inj + scal[2, o]
                        g = twice_slope(mixed)
                        a = g * g * (w_ref[half + at : half + at + GRID, cells] + (0.25 * rock) * direc)
                        local = local + rock * a
                        adj.append(a)
                    top, rest = split(jnp.concatenate(adj, axis=1))
                    t_ref[at : at + GRID], u_ref[at : at + GRID] = top, rest
                    at += GRID
            local_ref[plane] = local
        both = dot(t_ref[...], tab[384:640])
        z = both[:, :LANES] + both[:, LANES:] + dot(u_ref[...], tab[384:640, :LANES])
        top, rest = split(z)
        at = 0
        for plane in range(2):
            for kappa in kappas:
                for pair in range(2):
                    z_ref[4 * kappa + 2 * plane + pair, :GRID] = top[at : at + GRID]
                    z_ref[4 * kappa + 2 * plane + pair, GRID:] = rest[at : at + GRID]
                    at += GRID

    steps = KAPPAS // GROUP
    front(0)
    copy.wait()
    for k in range(steps):
        if k + 1 < steps:
            front(k + 1)
        back(k)

    for kappa in range(KAPPAS):
        v = dot(tab[640:736], jnp.concatenate([z_ref[4 * kappa + k] for k in range(4)], axis=1))
        v = v[:48] + v[48:]
        for plane in range(2):
            first, second = (v[:, k * LANES : (k + 1) * LANES] for k in (2 * plane, 2 * plane + 1))
            w = jnp.where(
                low,
                first[:HALF] + pltpu.roll(first[HALF:], LANES - PAIR, 1),
                jnp.where(high, pltpu.roll(second[:HALF], PAIR, 1) + second[HALF:], zero),
            )
            for bi in range(3):
                out_ref[kappa, :, plane, bi * LANES : (bi + 1) * LANES] = w[8 * bi : 8 * bi + 8]


GROUP = 1


def pull_kernel(r_ref, t_ref, across, ed, out_ref):
    beta = lax.rem(lax.axis_index("pen"), BETAS)
    fields = [
        jnp.concatenate([r_ref[:, k, bi * LANES : (bi + 1) * LANES] for k in range(2)], axis=0)
        for bi in range(3)
    ]
    g = left(across[beta, 256:384], across[beta, 384:512], jnp.concatenate(fields, axis=1))
    real = part_mask((OWNERS, LANES))
    parts = []
    for bi in range(3):
        t = t_ref[:, bi, :]
        fr, fi = g[:64, bi * LANES : (bi + 1) * LANES], g[64:, bi * LANES : (bi + 1) * LANES]
        s = swap(fi, real)
        v = fr + jnp.where(real, s, -s)
        parts += [t * v, t * swap(v, real)]
    q = right_exact(jnp.concatenate(parts, axis=1), ed[...])
    h = left(across[beta, 512:640], across[beta, 640:768], jnp.concatenate([q[:, :LANES], q[:, LANES:]], axis=0))
    for source in range(2):
        out_ref[GRID * source : GRID * source + GRID] = h


def final_kernel(r_ref, tab, mine_ref, theirs_ref, out_ref):
    lane = lax.broadcasted_iota(jnp.int32, (BETAS, LANES), 1)
    rows = [[], []]
    total = []
    for plane in range(2):
        x = r_ref[pl.ds(plane, BETAS, stride=2), :]
        for k in range(1, 2 * KAPPAS):
            x = x + r_ref[pl.ds(2 * BETAS * k + plane, BETAS, stride=2), :]
        total.append(x)
    for part in range(2):
        for bi in range(3):
            x = jnp.zeros((BETAS, LANES), F32)
            for plane in range(2):
                at = plane * PAIR + part * HALF
                shift = (at - HALF * bi) % LANES
                moved = pltpu.roll(total[plane], shift, 1) if shift else total[plane]
                x = jnp.where((lane >= at) & (lane < at + HALF), moved, x)
            rows[part].append(x)
    top, rest = split(jnp.concatenate(rows[0] + rows[1], axis=0))
    y = dot(tab[384:512, :144], jnp.concatenate([top, top, rest], axis=0))
    top, rest = split(y)
    z = dot(jnp.concatenate([top, rest], axis=1), tab[0:256]) + dot(top, tab[256:384])
    for plane in range(2):
        out_ref[plane] = z[:, plane * GRID : (plane + 1) * GRID] + (mine_ref[plane] + theirs_ref[plane])


VMEM = pl.BlockSpec(memory_space=pltpu.VMEM)
SMEM = pl.BlockSpec(memory_space=pltpu.SMEM)
HBM = pl.BlockSpec(memory_space=pltpu.HBM)
PARAMS = dict(compiler_params=pltpu.CompilerParams(vmem_limit_bytes=40 * 1024 * 1024))


def field_call(*operands):
    return pl.pallas_call(
        field_kernel,
        out_shape=[
            jax.ShapeDtypeStruct((KAPPAS, BETAS, 2, 3 * LANES), F32),
            jax.ShapeDtypeStruct((2, GRID, GRID), F32),
        ],
        in_specs=[HBM] + [VMEM] * 5,
        out_specs=[VMEM] * 2,
        scratch_shapes=[pltpu.SMEM((3, CHANNELS), F32)]
        + [
            pltpu.VMEM((4 * KAPPAS, 2 * GRID, LANES), BF16),
            *[pltpu.VMEM((8 * GROUP * GRID, 2 * GRID), F32)] * 2,
            *[pltpu.VMEM((4 * GROUP * GRID, 2 * GRID), BF16)] * 4,
            pltpu.SemaphoreType.DMA,
        ],
        name="field",
        **PARAMS,
    )(*operands)


def shards(permeability, direction, injection, lift_rock, lift_well, spectral, pointwise, offsets):
    tab = {
        k: tuple(jnp.asarray(x) for x in v) if isinstance(v, tuple) else jnp.asarray(v)
        for k, v in TABLES.items()
    }
    inj = injection[0]

    send = pl.pallas_call(
        first_kernel,
        out_shape=jax.ShapeDtypeStruct((KAPPAS, BETAS, 8, LANES), F32),
        in_specs=[HBM] * 7,
        out_specs=VMEM,
        scratch_shapes=[
            *[pltpu.SMEM((CHANNELS,), F32)] * 2,
            pltpu.VMEM((2, CHANNELS, CHANNELS, spectral.shape[0]), F32),
            *[pltpu.VMEM((2, GRID, GRID), F32)] * 3,
            pltpu.VMEM((320, 2 * LANES), BF16),
            pltpu.VMEM((4, CHANNELS, LANES), F32),
            pltpu.SemaphoreType.DMA((7,)),
        ],
        name="first",
        compiler_params=pltpu.CompilerParams(vmem_limit_bytes=60 * 1024 * 1024),
    )(
        lift_rock, lift_well, spectral.transpose(1, 2, 3, 0),
        permeability, direction, inj, tab["first"],
    )
    send = send.reshape(OWNERS, 8, LANES)
    owned = lax.all_to_all(send, "pen", 0, 0, tiled=True)

    send, scal = pl.pallas_call(
        owners_kernel,
        out_shape=[
            jax.ShapeDtypeStruct((OWNERS, 2, 5 * LANES), F32),
            jax.ShapeDtypeStruct((3, CHANNELS), F32),
        ],
        in_specs=[VMEM, VMEM, VMEM, HBM, HBM, VMEM, VMEM],
        out_specs=[VMEM] * 2,
        scratch_shapes=[pltpu.SMEM((CHANNELS,), F32)] * 2 + [pltpu.SemaphoreType.DMA((2,))],
        name="owners",
        **PARAMS,
    )(
        owned, tab["across"], tab["eb"],
        lift_rock, lift_well, pointwise, offsets.reshape(1, CHANNELS),
    )
    got = lax.all_to_all(send, "pen", 0, 0, tiled=True)

    send, local = field_call(scal, got.reshape(KAPPAS, BETAS, 2, 5 * LANES), tab["field"], permeability, direction, inj)
    back = lax.all_to_all(send.reshape(OWNERS, 2, 3 * LANES), "pen", 0, 0, tiled=True)

    send = pl.pallas_call(
        pull_kernel,
        out_shape=jax.ShapeDtypeStruct((4 * OWNERS, LANES), F32),
        in_specs=[VMEM] * 4,
        out_specs=VMEM,
        name="pull",
        **PARAMS,
    )(back, owned, tab["across"], tab["ed"])
    send, held = lax.optimization_barrier((send, local))
    last = lax.all_to_all(send, ("src", "pen"), 0, 0, tiled=True)
    theirs = lax.ppermute(held, "src", [(0, 1), (1, 0)])

    return pl.pallas_call(
        final_kernel,
        out_shape=jax.ShapeDtypeStruct((2, GRID, GRID), F32),
        in_specs=[VMEM] * 4,
        out_specs=VMEM,
        name="final",
        **PARAMS,
    )(last, tab["final"], local, theirs)


TABLES = build_tables()


def solution(mesh):
    placed = (
        P("pen", None, None),
        P("pen", None, None),
        P("src", "pen", None, None),
        P(),
        P(),
        P("pen", None, None, None),
        P(),
        P(),
    )
    return jax.shard_map(
        shards, mesh=mesh, in_specs=placed, out_specs=P("pen", None, None), check_vma=False
    )
```

```python
import math

import jax
import jax.numpy as jnp
import ml_dtypes
import numpy as np
from jax import lax
from jax.experimental import pallas as pl
from jax.experimental.pallas import tpu as pltpu
from jax.sharding import PartitionSpec as P

MODES = 12
GRID = 128
LANES = 128
BETAS = 8
KAPPAS = 8
OWNERS = BETAS * KAPPAS
CHANNELS = 32
CH = CHANNELS // KAPPAS
HALF = 24
PAIR = 48
FIELD_ROWS = 864
F32 = jnp.float32
BF16 = jnp.bfloat16


def halves(table):
    top = np.asarray(table, np.float32).astype(ml_dtypes.bfloat16)
    rest = (np.asarray(table, np.float64) - top.astype(np.float64)).astype(np.float32)
    return top, rest.astype(ml_dtypes.bfloat16)


def signed(j):
    return np.where(j < MODES, j, j - 3 * MODES)


def build_tables():
    point = np.arange(GRID)
    angle = 2 * np.pi / GRID
    scale = 1.0 / math.sqrt(GRID**3)
    c = np.arange(MODES)
    weight = np.where(c == 0, 1.0, 2.0)
    cos_z = np.cos(angle * ((c[:, None] * point[None]) % GRID))
    sin_z = np.sin(angle * ((c[:, None] * point[None]) % GRID))
    b = np.arange(2 * MODES)
    turn = (signed(b)[:, None] * point[None]) % GRID
    cos_y, sin_y = np.cos(angle * turn), np.sin(angle * turn)
    re, im = slice(0, MODES), slice(MODES, HALF)

    za = np.zeros((GRID, 2 * LANES))
    za[:, 0:12], za[:, 12:24] = cos_z.T, -sin_z.T
    za[:, 128:140], za[:, 140:152] = -sin_z.T, -cos_z.T
    za *= scale

    order = (3 * np.arange(BETAS)[None, :] + np.arange(3)[:, None]).reshape(-1)
    ya = np.concatenate([cos_y[order], sin_y[order]], axis=1)

    first = np.zeros((320, 2 * LANES), ml_dtypes.bfloat16)
    first[0:128], first[128:256] = halves(za)
    first[256:280], first[288:312] = halves(ya)

    x_of = (2 * np.arange(64)[None, :] + np.arange(2)[:, None]).reshape(-1)
    xb = np.zeros((BETAS, 2 * OWNERS, GRID))
    for beta in range(BETAS):
        for slot in range(64):
            j = (beta - 3 * slot) % 8
            if j < 3:
                a = (3 * slot + j) // 8
                ang = angle * ((signed(np.array(a)) * x_of) % GRID)
                xb[beta, slot], xb[beta, 64 + slot] = np.cos(ang), np.sin(ang)
    xi = xb.transpose(0, 2, 1).copy()
    xp = xi.reshape(BETAS, 2, 64, 2 * OWNERS).transpose(0, 2, 1, 3).reshape(BETAS, GRID, 2 * OWNERS).copy()

    eb = np.zeros((2 * LANES, 3, 2, LANES))
    for bi in range(3):
        for ch in range(CH):
            for k in range(MODES):
                lr, li = bi * HALF + k, bi * HALF + MODES + k
                hr, hi = ch * HALF + k, ch * HALF + MODES + k
                for lane in (hr, hi):
                    eb[lr, bi, 0, lane] = 1
                    eb[LANES + li, bi, 0, lane] = 1
                sign = {hr: -1, hi: 1}
                for lane in (hr, hi):
                    eb[li, bi, 1, lane] = sign[lane]
                    eb[LANES + lr, bi, 1, lane] = -sign[lane]
    eb = eb.reshape(2 * LANES, 6 * LANES)

    zc = np.zeros((LANES, 2, GRID))
    for q in range(2):
        r, i = slice(q * HALF, q * HALF + MODES), slice(q * HALF + MODES, (q + 1) * HALF)
        rs, js = slice(PAIR + r.start, PAIR + r.stop), slice(PAIR + i.start, PAIR + i.stop)
        zc[r, q], zc[i, q] = weight[:, None] * cos_z, -weight[:, None] * sin_z
        zc[rs, q], zc[js, q] = -weight[:, None] * sin_z, -weight[:, None] * cos_z
    zh, zl = halves(zc.reshape(LANES, 2 * GRID) * scale)
    yh, yl = halves(np.concatenate([cos_y[order], sin_y[order]], axis=0))
    field = np.zeros((FIELD_ROWS, 2 * GRID), ml_dtypes.bfloat16)
    field[0:128], field[128:256], field[256:384] = zh, zh, zl
    field[384:640, :LANES], field[384:640, LANES:] = zh.T, zl.T
    field[640:688, :GRID], field[640:688, GRID:] = yh, yh
    field[688:736, :GRID] = yl
    field[736:864, 0:48], field[736:864, 48:96], field[736:864, 96:144] = yh.T, yl.T, yh.T

    ed = np.zeros((3, 2, LANES, 2, LANES))
    for bi in range(3):
        for ch in range(CH):
            for k in range(MODES):
                lr, li = bi * HALF + k, bi * HALF + MODES + k
                hr, hi = ch * HALF + k, ch * HALF + MODES + k
                ed[bi, 0, hr, 0, lr] = ed[bi, 0, hi, 0, lr] = 1
                ed[bi, 1, hr, 0, li], ed[bi, 1, hi, 0, li] = 1, -1
                ed[bi, 1, hr, 1, lr], ed[bi, 1, hi, 1, lr] = -1, 1
                ed[bi, 0, hr, 1, li] = ed[bi, 0, hi, 1, li] = 1
    ed = ed.reshape(6 * LANES, 2 * LANES)

    ze = np.zeros((LANES, 2, GRID))
    for q in range(2):
        at = q * PAIR
        ze[at : at + 12, q], ze[at + 12 : at + 24, q] = cos_z, -sin_z
        ze[at + 24 : at + 36, q], ze[at + 36 : at + 48, q] = -sin_z, -cos_z
    zh, zl = halves(ze.reshape(LANES, 2 * GRID) * scale)
    final = np.zeros((512, 2 * GRID), ml_dtypes.bfloat16)
    final[0:128], final[128:256], final[256:384] = zh, zh, zl
    final[384:512] = field[736:864]

    return dict(
        first=first, across=np.concatenate([h for t in (xi, xb, xp) for h in halves(t)], axis=1), field=field, final=final,
        eb=eb.astype(ml_dtypes.bfloat16), ed=ed.astype(ml_dtypes.bfloat16),
    )


def split(x):
    top = x.astype(BF16)
    return top, (x - top.astype(F32)).astype(BF16)


def dot(a, b):
    return lax.dot_general(a, b, (((1,), (0,)), ((), ())), preferred_element_type=F32)


def left(table_hi, table_lo, x):
    hi, lo = split(x)
    return dot(table_hi, hi) + dot(table_hi, lo) + dot(table_lo, hi)


def right(x, table_hi, table_lo):
    hi, lo = split(x)
    return dot(hi, table_hi) + dot(lo, table_hi) + dot(hi, table_lo)


def right_exact(x, table):
    hi, lo = split(x)
    return dot(hi, table) + dot(lo, table)


def part_mask(shape):
    lane = lax.broadcasted_iota(jnp.int32, shape, 1)
    return lax.rem(lane, HALF) < MODES


def swap(x, real):
    return jnp.where(real, pltpu.roll(x, LANES - MODES, 1), pltpu.roll(x, MODES, 1))


def first_kernel(
    rock_hbm, well_hbm, s_hbm, p_hbm, d_hbm, i_hbm, tab_hbm,
    out_ref, rock_ref, well_ref, s_ref, p_ref, d_ref, i_ref, tab, t_ref, sems,
):
    pairs = (
        (tab_hbm, tab), (p_hbm, p_ref), (d_hbm, d_ref), (i_hbm, i_ref),
        (rock_hbm, rock_ref), (well_hbm, well_ref), (s_hbm, s_ref),
    )
    copies = [pltpu.make_async_copy(src, dst, sems.at[k]) for k, (src, dst) in enumerate(pairs)]
    for copy in copies:
        copy.start()
    for copy in copies[:-1]:
        copy.wait()
    x = jnp.concatenate([r[k] for r in (p_ref, d_ref, i_ref) for k in range(2)], axis=0)
    z = right(x, tab[0:128], tab[128:256])
    cols = [
        jnp.concatenate([z[k * GRID : (k + 1) * GRID, :LANES], z[k * GRID : (k + 1) * GRID, LANES:]], axis=0)
        for k in range(6)
    ]
    v = left(tab[256:280], tab[288:312], jnp.concatenate(cols, axis=1))
    lane = lax.broadcasted_iota(jnp.int32, (BETAS, LANES), 1)
    piece = [
        [v[8 * bi : 8 * bi + 8, k * LANES : (k + 1) * LANES] for bi in range(3)] for k in range(6)
    ]
    rows = [pltpu.roll(piece[k][2], 96, 1) for k in range(6)]
    for bi in range(2):
        for third in range(3):
            moved = pltpu.roll(piece[5][bi], 120 - 8 * third, 1)
            rows[3 * bi + third] = jnp.where(lane >= 120, moved, rows[3 * bi + third])
        total = piece[0][bi]
        for k in range(1, 5):
            total = total + pltpu.roll(piece[k][bi], HALF * k, 1)
        rows.append(total)
    for r in range(8):
        for kappa in range(KAPPAS):
            out_ref[kappa, :, r, :] = rows[r]

    copies[-1].wait()
    for part in range(2):
        rock = s_ref[part, 0] * rock_ref[0]
        well = s_ref[part, 0] * well_ref[0]
        for i in range(1, CHANNELS):
            x = s_ref[part, i]
            rock = rock + x * rock_ref[i]
            well = well + x * well_ref[i]
        t_ref[part, :, : rock.shape[1]] = rock
        t_ref[2 + part, :, : rock.shape[1]] = well
    lane = lax.broadcasted_iota(jnp.int32, (KAPPAS, LANES), 1)
    block = [[jnp.zeros((KAPPAS, LANES), F32) for _ in range(9)] for _ in range(2)]
    for ch in range(CH):
        for part in range(2):
            slot = 2 * ch + part
            inside = (lane >= slot * MODES) & (lane < (slot + 1) * MODES)
            for kind in range(2):
                x = t_ref[2 * kind + part, pl.ds(ch, KAPPAS, stride=CH), :]
                for row in range(9):
                    shift = ((slot - row) * MODES) % LANES
                    moved = pltpu.roll(x, shift, 1) if shift else x
                    block[kind][row] = jnp.where(inside, moved, block[kind][row])
    for j in range(3):
        beta = lax.rem(3 * lax.axis_index("pen") + j, BETAS)
        for kind in range(2):
            for bi in range(3):
                r = 3 * kind + bi
                out_ref[:, beta, r, :] = out_ref[:, beta, r, :] + block[kind][3 * j + bi]


def owners_kernel(
    r_ref, across, eb, rock_hbm, well_hbm, mix_ref, off_ref, out_ref, scal_ref, rock_ref, well_ref, sems
):
    beta = lax.rem(lax.axis_index("pen"), BETAS)
    copies = [
        pltpu.make_async_copy(src, dst, sems.at[k])
        for k, (src, dst) in enumerate(((rock_hbm, rock_ref), (well_hbm, well_ref)))
    ]
    for copy in copies:
        copy.start()
    raw = [r_ref[:, r, :] for r in range(8)]
    lane = lax.broadcasted_iota(jnp.int32, (OWNERS, LANES), 1)

    def take(x, source, target, width, base):
        shift = (target - source) % LANES
        moved = pltpu.roll(x, shift, 1) if shift else x
        return jnp.where((lane >= target) & (lane < target + width), moved, base)

    planes = []
    for k in range(6):
        x = take(raw[k], 96, 48, HALF, jnp.zeros((OWNERS, LANES), F32))
        for bi in range(2):
            if k < 5:
                x = take(raw[6 + bi], HALF * k, HALF * bi, HALF, x)
            else:
                for third in range(3):
                    x = take(raw[3 * bi + third], 120, HALF * bi + 8 * third, 8, x)
        planes.append(x)
    fields = [jnp.concatenate(planes[2 * f : 2 * f + 2], axis=0) for f in range(3)]
    g = left(across[beta, 256:384], across[beta, 384:512], jnp.concatenate(fields, axis=1))
    wide = jnp.concatenate(
        [
            jnp.concatenate([g[k : k + 64, f * LANES : (f + 1) * LANES] for k in (0, 64)], axis=1)
            for f in range(3)
        ],
        axis=0,
    )
    wide = right_exact(wide, eb[...])
    pre = [wide[OWNERS * f : OWNERS * (f + 1)] for f in range(3)]
    real = part_mask((OWNERS, LANES))
    stack = []
    for bi in range(3):
        t, w = raw[bi], raw[3 + bi]
        ts, ws = swap(t, real), swap(w, real)
        lo, mid, hi = 2 * bi * LANES, (2 * bi + 1) * LANES, (2 * bi + 2) * LANES
        coeff = (
            t * pre[0][:, lo:mid] + ts * pre[0][:, mid:hi]
            + w * pre[2][:, lo:mid] + ws * pre[2][:, mid:hi]
        )
        tangent = t * pre[1][:, lo:mid] + ts * pre[1][:, mid:hi]
        for q in (coeff, 0.25 * tangent):
            s = swap(q, real)
            stack.append(jnp.concatenate([q, jnp.where(real, -s, s)], axis=0))
    o = left(across[beta, 0:128], across[beta, 128:256], jnp.concatenate(stack, axis=1))
    for plane in range(2):
        piece = [o[plane * 64 : plane * 64 + 64, k * LANES : (k + 1) * LANES] for k in range(6)]
        for k in range(5):
            spare = take(piece[5], HALF * k, 96, HALF, piece[k]) if k < CH else piece[k]
            out_ref[:, plane, k * LANES : (k + 1) * LANES] = spare
    for copy in copies:
        copy.wait()
    rock = mix_ref[0:1] * rock_ref[0]
    well = mix_ref[0:1] * well_ref[0]
    for i in range(1, CHANNELS):
        rock = rock + mix_ref[i : i + 1] * rock_ref[i]
        well = well + mix_ref[i : i + 1] * well_ref[i]
    scal_ref[0:1], scal_ref[1:2], scal_ref[2:3] = rock, well, off_ref[...]


ROOT = math.sqrt(2.0 / math.pi)
CUBIC = 0.044715


def twice_slope(x):
    square = x * x
    t = jnp.tanh(x * (ROOT + (ROOT * CUBIC) * square))
    return (1.0 + t) * (1.0 + (x * (ROOT + (3.0 * ROOT * CUBIC) * square)) * (1.0 - t))


def field_kernel(
    scal_hbm, r_ref, tab, p_ref, d_ref, i_ref,
    out_ref, local_ref, scal, z_ref, w0, w1, t0, t1, u0, u1, sem,
):
    copy = pltpu.make_async_copy(scal_hbm, scal, sem)
    copy.start()
    w_refs, t_refs, u_refs = (w0, w1), (t0, t1), (u0, u1)
    lane = lax.broadcasted_iota(jnp.int32, (HALF, LANES), 1)
    low, high = lane < PAIR, (lane >= PAIR) & (lane < 2 * PAIR)
    zero = jnp.zeros((HALF, LANES), F32)
    row = lax.broadcasted_iota(jnp.int32, (BETAS, LANES), 1)
    local_ref[...] = jnp.zeros_like(local_ref)

    def piece(kappa, plane, k):
        if k < 5:
            return r_ref[kappa, :, plane, k * LANES : (k + 1) * LANES]
        x = jnp.zeros((BETAS, LANES), F32)
        for q in range(CH):
            moved = pltpu.roll(r_ref[kappa, :, plane, q * LANES : (q + 1) * LANES], 32 + HALF * q, 1)
            x = jnp.where((row >= HALF * q) & (row < HALF * (q + 1)), moved, x)
        return x

    def front(k):
        kappas = [GROUP * k + m for m in range(GROUP)]
        w_ref = w_refs[k % 2]
        rhs = []
        for field in range(2):
            for plane in range(2):
                for kappa in kappas:
                    s = jnp.concatenate([piece(kappa, plane, bi * 2 + field) for bi in range(3)], axis=0)
                    right_pair = pltpu.roll(s, PAIR, 1)
                    left_pair = pltpu.roll(s, LANES - PAIR, 1)
                    rhs.append(
                        jnp.concatenate([jnp.where(low, s, zero), jnp.where(high, right_pair, zero)], axis=0)
                    )
                    rhs.append(
                        jnp.concatenate([jnp.where(low, left_pair, zero), jnp.where(high, s, zero)], axis=0)
                    )
        count = len(rhs)
        top, rest = split(jnp.concatenate(rhs, axis=1))
        y = dot(tab[736:864, :144], jnp.concatenate([top, top, rest], axis=0))
        top, rest = split(y)
        both = jnp.concatenate(
            [
                jnp.concatenate([h[:, c * LANES : (c + 1) * LANES] for h in (top, rest)], axis=1)
                for c in range(count)
            ],
            axis=0,
        )
        w_ref[...] = dot(both, tab[0:256]) + dot(both[:, :LANES], tab[256:384])

    def back(k):
        kappas = [GROUP * k + m for m in range(GROUP)]
        w_ref, t_ref, u_ref = w_refs[k % 2], t_refs[k % 2], u_refs[k % 2]
        half = 4 * GROUP * GRID
        at = 0
        for plane in range(2):
            perm, direc, inj = p_ref[plane], d_ref[plane], i_ref[plane]
            local = local_ref[plane]
            for kappa in kappas:
                for pair in range(2):
                    adj = []
                    for q in range(2):
                        o = kappa * CH + 2 * pair + q
                        rock = scal[0, o]
                        cells = slice(q * GRID, (q + 1) * GRID)
                        mixed = w_ref[at : at + GRID, cells] + rock * perm + scal[1, o] * inj + scal[2, o]
                        g = twice_slope(mixed)
                        a = g * g * (w_ref[half + at : half + at + GRID, cells] + (0.25 * rock) * direc)
                        local = local + rock * a
                        adj.append(a)
                    top, rest = split(jnp.concatenate(adj, axis=1))
                    t_ref[at : at + GRID], u_ref[at : at + GRID] = top, rest
                    at += GRID
            local_ref[plane] = local
        both = dot(t_ref[...], tab[384:640])
        z = both[:, :LANES] + both[:, LANES:] + dot(u_ref[...], tab[384:640, :LANES])
        top, rest = split(z)
        at = 0
        for plane in range(2):
            for kappa in kappas:
                for pair in range(2):
                    z_ref[4 * kappa + 2 * plane + pair, :GRID] = top[at : at + GRID]
                    z_ref[4 * kappa + 2 * plane + pair, GRID:] = rest[at : at + GRID]
                    at += GRID

    def finish(kappa):
        v = dot(tab[640:736], jnp.concatenate([z_ref[4 * kappa + k] for k in range(4)], axis=1))
        v = v[:48] + v[48:]
        for plane in range(2):
            first, second = (v[:, k * LANES : (k + 1) * LANES] for k in (2 * plane, 2 * plane + 1))
            w = jnp.where(
                low,
                first[:HALF] + pltpu.roll(first[HALF:], LANES - PAIR, 1),
                jnp.where(high, pltpu.roll(second[:HALF], PAIR, 1) + second[HALF:], zero),
            )
            for bi in range(3):
                out_ref[kappa, :, plane, bi * LANES : (bi + 1) * LANES] = w[8 * bi : 8 * bi + 8]

    steps = KAPPAS // GROUP
    front(0)
    copy.wait()
    for k in range(steps):
        if k + 1 < steps:
            front(k + 1)
        back(k)
        if k > 0:
            finish(k - 1)
    finish(steps - 1)


GROUP = 1


def pull_kernel(r_ref, t_ref, across, ed, out_ref):
    beta = lax.rem(lax.axis_index("pen"), BETAS)
    fields = [
        jnp.concatenate([r_ref[:, k, bi * LANES : (bi + 1) * LANES] for k in range(2)], axis=0)
        for bi in range(3)
    ]
    g = left(across[beta, 256:384], across[beta, 384:512], jnp.concatenate(fields, axis=1))
    real = part_mask((OWNERS, LANES))
    parts = []
    for bi in range(3):
        t = t_ref[:, bi, :]
        fr, fi = g[:64, bi * LANES : (bi + 1) * LANES], g[64:, bi * LANES : (bi + 1) * LANES]
        s = swap(fi, real)
        v = fr + jnp.where(real, s, -s)
        parts += [t * v, t * swap(v, real)]
    q = right_exact(jnp.concatenate(parts, axis=1), ed[...])
    h = left(across[beta, 512:640], across[beta, 640:768], jnp.concatenate([q[:, :LANES], q[:, LANES:]], axis=0))
    for source in range(2):
        out_ref[GRID * source : GRID * source + GRID] = h


def final_kernel(r_ref, tab, mine_ref, theirs_ref, out_ref):
    lane = lax.broadcasted_iota(jnp.int32, (BETAS, LANES), 1)
    rows = [[], []]
    total = []
    for plane in range(2):
        x = r_ref[pl.ds(plane, BETAS, stride=2), :]
        for k in range(1, 2 * KAPPAS):
            x = x + r_ref[pl.ds(2 * BETAS * k + plane, BETAS, stride=2), :]
        total.append(x)
    for part in range(2):
        for bi in range(3):
            x = jnp.zeros((BETAS, LANES), F32)
            for plane in range(2):
                at = plane * PAIR + part * HALF
                shift = (at - HALF * bi) % LANES
                moved = pltpu.roll(total[plane], shift, 1) if shift else total[plane]
                x = jnp.where((lane >= at) & (lane < at + HALF), moved, x)
            rows[part].append(x)
    top, rest = split(jnp.concatenate(rows[0] + rows[1], axis=0))
    y = dot(tab[384:512, :144], jnp.concatenate([top, top, rest], axis=0))
    top, rest = split(y)
    z = dot(jnp.concatenate([top, rest], axis=1), tab[0:256]) + dot(top, tab[256:384])
    for plane in range(2):
        out_ref[plane] = z[:, plane * GRID : (plane + 1) * GRID] + (mine_ref[plane] + theirs_ref[plane])


VMEM = pl.BlockSpec(memory_space=pltpu.VMEM)
SMEM = pl.BlockSpec(memory_space=pltpu.SMEM)
HBM = pl.BlockSpec(memory_space=pltpu.HBM)
PARAMS = dict(compiler_params=pltpu.CompilerParams(vmem_limit_bytes=40 * 1024 * 1024))


def field_call(*operands):
    return pl.pallas_call(
        field_kernel,
        out_shape=[
            jax.ShapeDtypeStruct((KAPPAS, BETAS, 2, 3 * LANES), F32),
            jax.ShapeDtypeStruct((2, GRID, GRID), F32),
        ],
        in_specs=[HBM] + [VMEM] * 5,
        out_specs=[VMEM] * 2,
        scratch_shapes=[pltpu.SMEM((3, CHANNELS), F32)]
        + [
            pltpu.VMEM((4 * KAPPAS, 2 * GRID, LANES), BF16),
            *[pltpu.VMEM((8 * GROUP * GRID, 2 * GRID), F32)] * 2,
            *[pltpu.VMEM((4 * GROUP * GRID, 2 * GRID), BF16)] * 4,
            pltpu.SemaphoreType.DMA,
        ],
        name="field",
        **PARAMS,
    )(*operands)


def shards(permeability, direction, injection, lift_rock, lift_well, spectral, pointwise, offsets):
    tab = {
        k: tuple(jnp.asarray(x) for x in v) if isinstance(v, tuple) else jnp.asarray(v)
        for k, v in TABLES.items()
    }
    inj = injection[0]

    send = pl.pallas_call(
        first_kernel,
        out_shape=jax.ShapeDtypeStruct((KAPPAS, BETAS, 8, LANES), F32),
        in_specs=[HBM] * 7,
        out_specs=VMEM,
        scratch_shapes=[
            *[pltpu.SMEM((CHANNELS,), F32)] * 2,
            pltpu.VMEM((2, CHANNELS, CHANNELS, spectral.shape[0]), F32),
            *[pltpu.VMEM((2, GRID, GRID), F32)] * 3,
            pltpu.VMEM((320, 2 * LANES), BF16),
            pltpu.VMEM((4, CHANNELS, LANES), F32),
            pltpu.SemaphoreType.DMA((7,)),
        ],
        name="first",
        compiler_params=pltpu.CompilerParams(vmem_limit_bytes=60 * 1024 * 1024),
    )(
        lift_rock, lift_well, spectral.transpose(1, 2, 3, 0),
        permeability, direction, inj, tab["first"],
    )
    send = send.reshape(OWNERS, 8, LANES)
    owned = lax.all_to_all(send, "pen", 0, 0, tiled=True)

    send, scal = pl.pallas_call(
        owners_kernel,
        out_shape=[
            jax.ShapeDtypeStruct((OWNERS, 2, 5 * LANES), F32),
            jax.ShapeDtypeStruct((3, CHANNELS), F32),
        ],
        in_specs=[VMEM, VMEM, VMEM, HBM, HBM, VMEM, VMEM],
        out_specs=[VMEM] * 2,
        scratch_shapes=[pltpu.SMEM((CHANNELS,), F32)] * 2 + [pltpu.SemaphoreType.DMA((2,))],
        name="owners",
        **PARAMS,
    )(
        owned, tab["across"], tab["eb"],
        lift_rock, lift_well, pointwise, offsets.reshape(1, CHANNELS),
    )
    got = lax.all_to_all(send, "pen", 0, 0, tiled=True)

    send, local = field_call(scal, got.reshape(KAPPAS, BETAS, 2, 5 * LANES), tab["field"], permeability, direction, inj)
    back = lax.all_to_all(send.reshape(OWNERS, 2, 3 * LANES), "pen", 0, 0, tiled=True)

    send = pl.pallas_call(
        pull_kernel,
        out_shape=jax.ShapeDtypeStruct((4 * OWNERS, LANES), F32),
        in_specs=[VMEM] * 4,
        out_specs=VMEM,
        name="pull",
        **PARAMS,
    )(back, owned, tab["across"], tab["ed"])
    send, held = lax.optimization_barrier((send, local))
    last = lax.all_to_all(send, ("src", "pen"), 0, 0, tiled=True)
    theirs = lax.ppermute(held, "src", [(0, 1), (1, 0)])

    return pl.pallas_call(
        final_kernel,
        out_shape=jax.ShapeDtypeStruct((2, GRID, GRID), F32),
        in_specs=[VMEM] * 4,
        out_specs=VMEM,
        name="final",
        **PARAMS,
    )(last, tab["final"], local, theirs)


TABLES = build_tables()


def solution(mesh):
    placed = (
        P("pen", None, None),
        P("pen", None, None),
        P("src", "pen", None, None),
        P(),
        P(),
        P("pen", None, None, None),
        P(),
        P(),
    )
    return jax.shard_map(
        shards, mesh=mesh, in_specs=placed, out_specs=P("pen", None, None), check_vma=False
    )
```
